512 devices in a mesh: grp: 8 (over z), dev: 64 (over x, y, core).
Axes of the slice: x: 4, y: 8, z: 8, core: 2. Of those that a mesh axis runs over, the one named last changes fastest.
Arguments:
- snapshots: float32 [262144, 128], P(('grp', 'dev')), may hold values from -16.5 to 16.5
- basis: float32 [262144, 128], P(('grp', 'dev')), may hold values from -1.4 to 1.4
Outputs:
- modes: float32 [262144, 128], P(('grp', 'dev'))
- factor: float32 [128, 128], replicated
- coefficients: float32 [128, 128], replicated
The draws below stay inside these ranges and needn't reach their ends.
All inputs are finite; a program needn't handle non-finite values.
Results may differ from the reference program's by a relative error of at most 0.0003.
Values sent between devices are 32-bit elements; how exact they have to be, the bound alone decides.
No kernel may reach another device: no remote copies, remote signals or barrier semaphores. Data moves between devices by JAX's collectives and lax.ppermute only.
A program may use at most 64 MiB of HBM per device.

```python
import math
import jax
import jax.numpy as jnp
from jax import lax

K = 128
B = 128
ROWS = 262144


def parity_of(values):
    folded = jnp.bitwise_xor(values, jnp.right_shift(values, 16))
    folded = jnp.bitwise_xor(folded, jnp.right_shift(folded, 8))
    folded = jnp.bitwise_xor(folded, jnp.right_shift(folded, 4))
    folded = jnp.bitwise_xor(folded, jnp.right_shift(folded, 2))
    folded = jnp.bitwise_xor(folded, jnp.right_shift(folded, 1))
    return jnp.bitwise_and(folded, 1)


def walsh_table(row_index, column_masks):
    parity_bits = parity_of(jnp.bitwise_and(row_index[:, None], column_masks[None, :]))
    return 1.0 - 2.0 * parity_bits.astype(jnp.float32)


def basis_field(key):
    base_key = jax.random.fold_in(key, 7001)
    key_mult, key_rows, key_drift, key_noise = jax.random.split(base_key, 4)
    multiplier = 2 * jax.random.randint(key_mult, (), 0, 4096, dtype=jnp.int32) + 1
    column_index = jnp.arange(1, B + 1, dtype=jnp.int32)
    column_masks = jnp.bitwise_and(column_index * multiplier, ROWS - 1)
    row_index = jnp.arange(ROWS, dtype=jnp.int32)
    row_sign = 1.0 - 2.0 * jax.random.randint(key_rows, (ROWS, 1), 0, 2, dtype=jnp.int32).astype(jnp.float32)
    walsh = walsh_table(row_index, column_masks)
    drift = jnp.exp(jax.random.uniform(key_drift, (1, B), jnp.float32, math.log(0.01), math.log(0.05)))
    noise = 0.1 * jax.random.truncated_normal(key_noise, -3.0, 3.0, (ROWS, B), jnp.float32)
    return row_sign * (walsh + drift * jnp.roll(walsh, -1, axis=1)) + noise


def draw_basis(key, part):
    return basis_field(key)


def draw_snapshots(key, part):
    basis = basis_field(key)
    base_key = jax.random.fold_in(key, 7002)
    key_list = jax.random.split(base_key, 9)
    first_pick = jax.random.randint(key_list[0], (K,), 0, B, dtype=jnp.int32)
    second_pick = jnp.remainder(first_pick + jax.random.randint(key_list[1], (K,), 1, B, dtype=jnp.int32), B)
    sign_pair = 1.0 - 2.0 * jax.random.randint(key_list[2], (2, K), 0, 2, dtype=jnp.int32).astype(jnp.float32)
    amplitude = jnp.exp(jax.random.uniform(key_list[3], (2, K), jnp.float32, math.log(0.5), math.log(1.5))) * sign_pair
    in_span = jnp.take(basis, first_pick, axis=1) * amplitude[0][None, :] + jnp.take(basis, second_pick, axis=1) * amplitude[1][None, :]
    load_size = jnp.exp(jax.random.uniform(key_list[5], (1, K), jnp.float32, math.log(0.5), math.log(2.0)))
    common = jax.random.truncated_normal(key_list[4], -4.0, 4.0, (ROWS, 1), jnp.float32)
    load_sign = 1.0 - 2.0 * jax.random.randint(jax.random.fold_in(key_list[5], 3), (1, K), 0, 2, dtype=jnp.int32).astype(jnp.float32)
    loading = load_size * load_sign
    own_part = jax.random.truncated_normal(key_list[6], -4.0, 4.0, (ROWS, K), jnp.float32)
    ranked = jax.random.permutation(key_list[7], K).astype(jnp.float32)
    jitter = jax.random.uniform(key_list[8], (K,), jnp.float32, 0.0, 1.0)
    levels = jnp.exp(math.log(0.005) * (ranked + jitter) / K)
    return in_span + common * loading + own_part * levels[None, :]


def setup_inputs(seed: int = 0) -> dict:
    keys = jax.random.split(jax.random.key(seed), 3)
    snapshots = draw_snapshots(jax.random.fold_in(keys[2], 71), 0)
    basis = draw_basis(jax.random.fold_in(keys[2], 71), 0)
    return {"snapshots": snapshots, "basis": basis}


def cross_product(left, right):
    return jnp.einsum('rb,rk->bk', left, right, precision=lax.Precision.HIGHEST)

def apply_basis(basis, coef):
    return jnp.dot(basis, coef, precision=lax.Precision.HIGHEST)

def cholesky_upper(gram):
    size_n = gram.shape[0]
    column_ids = jnp.arange(size_n, dtype=jnp.int32)

    def column_step(step, carry):
        work, upper = carry
        row_vals = lax.dynamic_slice_in_dim(work, step, 1, 0)[0]
        pivot = jnp.sqrt(jnp.sum(jnp.where(column_ids == step, row_vals, 0.0)))
        row_new = jnp.where(column_ids >= step, row_vals / pivot, 0.0)
        upper = upper + jnp.where((column_ids == step)[:, None], row_new[None, :], 0.0)
        work = work - row_new[:, None] * row_new[None, :]
        return (work, upper)
    start = (gram, jnp.zeros_like(gram))
    return lax.fori_loop(0, size_n, column_step, start)[1]

def upper_inverse(gram):
    upper_part = cholesky_upper(gram)
    size_n = gram.shape[0]
    column_ids = jnp.arange(size_n, dtype=jnp.int32)

    def row_step(turn, inverse):
        row_at = size_n - 1 - turn
        row_vals = lax.dynamic_slice_in_dim(upper_part, row_at, 1, 0)[0]
        diag_val = jnp.sum(jnp.where(column_ids == row_at, row_vals, 0.0))
        off_diag = jnp.where(column_ids > row_at, row_vals, 0.0)
        unit_row = jnp.where(column_ids == row_at, 1.0, 0.0).astype(gram.dtype)
        new_row = (unit_row - jnp.dot(off_diag, inverse, precision=lax.Precision.HIGHEST)) / diag_val
        return inverse + jnp.where((column_ids == row_at)[:, None], new_row[None, :], 0.0)
    inverse = lax.fori_loop(0, size_n, row_step, jnp.zeros_like(gram))
    return (upper_part, inverse)

def reference(snapshots, basis):
    coef_one = cross_product(basis, snapshots) / ROWS
    first = snapshots - apply_basis(basis, coef_one)
    coef_two = cross_product(basis, first) / ROWS
    second = first - apply_basis(basis, coef_two)
    upper_one, inv_one = upper_inverse(cross_product(second, second) / ROWS)
    middle = apply_basis(second, inv_one)
    upper_two, inv_two = upper_inverse(cross_product(middle, middle) / ROWS)
    modes = apply_basis(middle, inv_two)
    factor = jnp.dot(upper_two, upper_one, precision=lax.Precision.HIGHEST)
    return (modes, factor, coef_one + coef_two)
```

```python
import functools

import jax
import jax.numpy as jnp
from jax import lax
from jax.experimental import pallas as pl
from jax.experimental.pallas import tpu as pltpu
from jax.sharding import PartitionSpec as P

HIGHEST = lax.Precision.HIGHEST
F32, BF16 = jnp.float32, jnp.bfloat16
N = 128
TILE = 8
TILES = N // TILE
PIECE = 2 * TILE


def two_sum(a, b):
    s = a + b
    t = s - a
    return s, (a - (s - t)) + (b - t)


def pair_sum(a, b):
    s, e = two_sum(a[0], b[0])
    return s, e + (a[1] + b[1])


def normal(a):
    s = a[0] + a[1]
    return s, a[1] - (s - a[0])


def dot_t(a, b, precision=None):
    return lax.dot_general(
        a, b, (((0,), (0,)), ((), ())), precision=precision, preferred_element_type=F32
    )


def dot(a, b, precision=None):
    return jnp.dot(a, b, precision=precision, preferred_element_type=F32)


def slices(hi, lo, axis, count, shift):
    step = jnp.max(jnp.abs(hi), axis=axis, keepdims=True) * (2.0**shift)
    first = (hi + step) - step
    rest = hi - first
    step = step * 2.0**-8
    second = (rest + step) - step
    rest = rest - second
    if lo is not None:
        rest = rest + lo
    out = [first.astype(BF16), second.astype(BF16)]
    while len(out) < count:
        part = rest.astype(BF16)
        rest = rest - part.astype(F32)
        out.append(part)
    return out


def exact_dot(left, right):
    wide = jnp.concatenate(left, axis=1)
    tall = jnp.concatenate(right[::-1], axis=0)
    n = len(left)
    terms = [dot(wide[:, : N * k], tall[N * (n - k) :, :]) for k in range(1, n + 1)]
    low = terms[-1]
    for t in terms[-2:1:-1]:
        low = low + t
    s, e = two_sum(terms[0], terms[1])
    return s, e + low


def local_kernel(snap_ref, basis_ref, out_ref):
    z = jnp.concatenate([basis_ref[...], snap_ref[...]], axis=1)
    a, b, c, d = slices(z, None, 0, 4, 17)
    main = dot_t(a, a)
    low_1 = dot_t(a, b)
    low_2 = dot_t(a, c) + 0.5 * dot_t(b, b)
    low_3 = dot_t(a, d) + dot_t(b, c)
    low_4 = dot_t(b, d) + 0.5 * dot_t(c, c)
    half = low_1 + (low_2 + (low_3 + low_4))
    hi, lo = two_sum(main, half + half.T)
    scale = 2.0**-18
    blocks = ((0, 0), (0, 1), (1, 1))
    for i, (r, s) in enumerate(blocks):
        for j, part in enumerate((hi, lo)):
            block = part[r * N : (r + 1) * N, s * N : (s + 1) * N]
            out_ref[i * TILES : (i + 1) * TILES, j * TILE : (j + 1) * TILE, :] = (
                block * scale
            ).reshape(TILES, TILE, N)
    used = len(blocks) * TILES
    out_ref[used:, :, :] = jnp.zeros_like(out_ref[used:, :, :])


def local_products(snapshots, basis, pieces):
    return pl.pallas_call(
        local_kernel,
        out_shape=jax.ShapeDtypeStruct((pieces, PIECE, N), F32),
        compiler_params=pltpu.CompilerParams(vmem_limit_bytes=32 << 20),
    )(snapshots, basis)


def sum_kernel(in_ref, out_ref):
    parts = [(in_ref[i, :TILE, :], in_ref[i, TILE:, :]) for i in range(in_ref.shape[0])]
    while len(parts) > 1:
        parts = [pair_sum(parts[i], parts[i + 1]) for i in range(0, len(parts), 2)]
    hi, lo = parts[0]
    for i in range(out_ref.shape[0]):
        out_ref[i, :TILE, :] = hi
        out_ref[i, TILE:, :] = lo


def sum_and_copy(parts, copies):
    return pl.pallas_call(
        sum_kernel,
        out_shape=jax.ShapeDtypeStruct((copies, PIECE, N), F32),
        compiler_params=pltpu.CompilerParams(vmem_limit_bytes=32 << 20),
    )(parts)


def factor_inverse(gram, scratch):
    sub = lax.broadcasted_iota(jnp.int32, (TILE, N), 0)
    lane = lax.broadcasted_iota(jnp.int32, (TILE, N), 1)
    work = gram
    inv = jnp.where(
        lax.broadcasted_iota(jnp.int32, (N, N), 0)
        == lax.broadcasted_iota(jnp.int32, (N, N), 1),
        1.0,
        0.0,
    ).astype(F32)
    upper_rows, inv_rows = [], []
    for p in range(TILES):
        at = p * TILE
        rows = work[:TILE, :]
        irow = inv[:TILE, :]
        d = {}
        for j in range(TILE):
            col = jnp.broadcast_to(rows[:, at + j : at + j + 1], (TILE, N))
            for i in range(j + 1):
                d[i, j] = jnp.broadcast_to(col[i : i + 1, :], (TILE, N))
        r = []
        for k in range(TILE):
            piv = d[k, k]
            y = lax.rsqrt(piv)
            y = y * (1.5 - 0.5 * piv * y * y)
            r.append(y)
            for j in range(k + 1, TILE):
                d[k, j] = d[k, j] * y
            for i in range(k + 1, TILE):
                for j in range(i, TILE):
                    d[i, j] = d[i, j] - d[k, i] * d[k, j]
        li = {}
        for j in range(TILE):
            li[j, j] = r[j]
            for i in range(j + 1, TILE):
                acc = d[j, i] * li[j, j]
                for k in range(j + 1, i):
                    acc = acc + d[k, i] * li[k, j]
                li[i, j] = -(acc * r[i])
        new_u = jnp.zeros((TILE, N), F32)
        new_i = jnp.zeros((TILE, N), F32)
        for k in range(TILE):
            colk = jnp.zeros((TILE, N), F32)
            for i in range(k, TILE):
                colk = jnp.where(sub == i, li[i, k], colk)
            new_u = new_u + colk * jnp.broadcast_to(rows[k : k + 1, :], (TILE, N))
            new_i = new_i + colk * jnp.broadcast_to(irow[k : k + 1, :], (TILE, N))
        new_u = jnp.where(lane >= at + sub, new_u, 0.0)
        upper_rows.append(new_u)
        inv_rows.append(new_i)
        if p + 1 < TILES:
            both = jnp.concatenate([new_u, new_i], axis=1)
            b1 = both.astype(BF16)
            rest = both - b1.astype(F32)
            b2 = rest.astype(BF16)
            b3 = (rest - b2.astype(F32)).astype(BF16)
            f1, f2, f3 = b1.astype(F32), b2.astype(F32), b3.astype(F32)
            left = jnp.concatenate([f[:, :N] for f in (f1, f1, f2, f1, f2, f3)], axis=0)
            right = jnp.concatenate([f1, f2, f1, f3, f2, f1], axis=0).astype(BF16)
            left = left.T.astype(BF16)[at + TILE :, :]
            upd = dot(left, right)
            work = work[TILE:, :] - upd[:, :N]
            inv = inv[TILE:, :] - upd[:, N:]
    return jnp.concatenate(upper_rows, axis=0), jnp.concatenate(inv_rows, axis=0)


def final_kernel(sums_ref, snap_ref, basis_ref, modes_ref, factor_ref, coef_ref, scratch):
    def pair(i):
        part = sums_ref[i * TILES : (i + 1) * TILES, :, :]
        return part[:, :TILE, :].reshape(N, N), part[:, TILE:, :].reshape(N, N)

    basis_gram, cross, snap_gram = pair(0), pair(1), pair(2)
    coef_two = cross[0] - dot(basis_gram[0], cross[0], HIGHEST)
    coef = cross[0] + coef_two
    coef_ref[...] = coef
    second = snap_ref[...] - dot(basis_ref[...], coef, HIGHEST)

    g_c = exact_dot(slices(*basis_gram, 1, 5, 16), slices(coef, None, 0, 5, 16))
    held = pair_sum((2.0 * cross[0], 2.0 * cross[1]), (-g_c[0], -g_c[1]))
    held = normal(held)
    c_h = exact_dot(slices(coef.T, None, 1, 5, 16), slices(*held, 0, 5, 16))
    c_h = pair_sum((0.5 * c_h[0], 0.5 * c_h[1]), (0.5 * c_h[0].T, 0.5 * c_h[1].T))
    gram_one = normal(pair_sum(snap_gram, (-c_h[0], -c_h[1])))

    upper_one, inv_one_t = factor_inverse(gram_one[0], scratch)
    inv_one = inv_one_t.T
    g_i = exact_dot(slices(*gram_one, 1, 5, 16), slices(inv_one, None, 0, 5, 16))
    g_i = normal(g_i)
    i_g_i = exact_dot(slices(inv_one_t, None, 1, 5, 16), slices(*g_i, 0, 5, 16))
    gram_two = i_g_i[0] + i_g_i[1]
    upper_two, inv_two_t = factor_inverse(gram_two, scratch)
    factor_ref[...] = dot(upper_two, upper_one, HIGHEST)
    both = dot(inv_one, inv_two_t.T, HIGHEST)
    modes_ref[...] = dot(second, both, HIGHEST)


def finish(sums, snapshots, basis):
    rows = snapshots.shape[0]
    return pl.pallas_call(
        final_kernel,
        out_shape=(
            jax.ShapeDtypeStruct((rows, N), F32),
            jax.ShapeDtypeStruct((N, N), F32),
            jax.ShapeDtypeStruct((N, N), F32),
        ),
        scratch_shapes=[pltpu.VMEM((N, N), F32)],
        compiler_params=pltpu.CompilerParams(vmem_limit_bytes=48 << 20),
    )(sums, snapshots, basis)


def body(snapshots, basis):
    group, many = lax.axis_size("grp"), lax.axis_size("dev")
    local = local_products(snapshots, basis, many)
    parts = lax.all_to_all(local, "dev", 0, 0)
    mine = sum_and_copy(parts, group)
    parts = lax.all_to_all(mine, "grp", 0, 0)
    mine = sum_and_copy(parts, many)
    sums = lax.all_to_all(mine, "dev", 0, 0)
    return finish(sums, snapshots, basis)


def solution(mesh):
    return jax.shard_map(
        body,
        mesh=mesh,
        in_specs=(P(("grp", "dev"), None), P(("grp", "dev"), None)),
        out_specs=(P(("grp", "dev"), None), P(), P()),
        check_vma=False,
    )
```

```python
import functools

import jax
import jax.numpy as jnp
from jax import lax
from jax.experimental import pallas as pl
from jax.experimental.pallas import tpu as pltpu
from jax.sharding import PartitionSpec as P

HIGHEST = lax.Precision.HIGHEST
F32, BF16 = jnp.float32, jnp.bfloat16
N = 128
TILE = 8
TILES = N // TILE


def two_sum(a, b):
    s = a + b
    t = s - a
    return s, (a - (s - t)) + (b - t)


def pair_sum(a, b):
    s, e = two_sum(a[0], b[0])
    return s, e + (a[1] + b[1])


def normal(a):
    s = a[0] + a[1]
    return s, a[1] - (s - a[0])


def dot_t(a, b, precision=None):
    return lax.dot_general(
        a, b, (((0,), (0,)), ((), ())), precision=precision, preferred_element_type=F32
    )


def dot(a, b, precision=None):
    return jnp.dot(a, b, precision=precision, preferred_element_type=F32)


def slices(hi, lo, axis, count, shift):
    step = jnp.max(jnp.abs(hi), axis=axis, keepdims=True) * (2.0**shift)
    first = (hi + step) - step
    rest = hi - first
    step = step * 2.0**-8
    second = (rest + step) - step
    rest = rest - second
    if lo is not None:
        rest = rest + lo
    out = [first.astype(BF16), second.astype(BF16)]
    while len(out) < count:
        part = rest.astype(BF16)
        rest = rest - part.astype(F32)
        out.append(part)
    return out


def exact_dot(left, right):
    wide = jnp.concatenate(left, axis=1)
    tall = jnp.concatenate(right[::-1], axis=0)
    n = len(left)
    terms = [dot(wide[:, : N * k], tall[N * (n - k) :, :]) for k in range(1, n + 1)]
    low = terms[-1]
    for t in terms[-2:1:-1]:
        low = low + t
    s, e = two_sum(terms[0], terms[1])
    return s, e + low


def grid(rows=N):
    return (
        lax.broadcasted_iota(jnp.int32, (rows, N), 0),
        lax.broadcasted_iota(jnp.int32, (rows, N), 1),
    )


def put_diagonal(rest, diagonal):
    row, col = grid(N // 2)
    near = pltpu.roll(diagonal[N // 2 :, :], N - N // 4, 1)
    far = pltpu.roll(diagonal[: N // 2, :], N // 2, 1)
    top = jnp.where(col == row + N // 4, near, rest[: N // 2, :])
    top = jnp.where(col == row + N // 2, far, top)
    return jnp.concatenate([top, rest[N // 2 :, :]], axis=0)


def take_diagonal(rest):
    row, col = grid(N // 2)
    top = rest[: N // 2, :]
    near, far = col == row + N // 4, col == row + N // 2
    first = pltpu.roll(jnp.where(far, top, 0.0), N // 2, 1)
    last = pltpu.roll(jnp.where(near, top, 0.0), N // 4, 1)
    top = jnp.where(near | far, 0.0, top)
    return (
        jnp.concatenate([first, last], axis=0),
        jnp.concatenate([top, rest[N // 2 :, :]], axis=0),
    )


def pack(hi, lo):
    hi, lo = hi.reshape(TILES, TILE, N), lo.reshape(TILES, TILE, N)
    upper = lax.broadcasted_iota(jnp.int32, hi.shape, 1) < TILE // 2
    even = jnp.where(upper, hi, pltpu.roll(lo, TILE // 2, 1))
    odd = jnp.where(upper, pltpu.roll(hi, TILE // 2, 1), lo)
    return jnp.stack([even, odd], axis=1).reshape(2 * TILES, TILE, N)


def unpack(pieces):
    pieces = pieces.reshape(TILES, 2, TILE, N)
    even, odd = pieces[:, 0], pieces[:, 1]
    upper = lax.broadcasted_iota(jnp.int32, even.shape, 1) < TILE // 2
    hi = jnp.where(upper, even, pltpu.roll(odd, TILE // 2, 1))
    lo = jnp.where(upper, pltpu.roll(even, TILE // 2, 1), odd)
    return hi.reshape(N, N), lo.reshape(N, N)


def local_kernel(share, total, snap_hbm, basis_hbm, out_ref, z_ref, sem):
    copies = [
        pltpu.make_async_copy(basis_hbm, z_ref.at[:, :N], sem.at[0]),
        pltpu.make_async_copy(snap_hbm, z_ref.at[:, N:], sem.at[1]),
    ]
    for copy in copies:
        copy.start()
    for copy in copies:
        copy.wait()
    a, b, c, d = slices(z_ref[...], None, 0, 4, 17)
    main = dot_t(a, a)
    low_1 = dot_t(a, b)
    low_2 = dot_t(a, c) + 0.5 * dot_t(b, b)
    low_3 = dot_t(a, d) + dot_t(b, c)
    low_4 = dot_t(b, d) + 0.5 * dot_t(c, c)
    half = low_1 + (low_2 + (low_3 + low_4))
    hi, lo = two_sum(main, half + half.T)
    hi, lo = hi * (1.0 / total), lo * (1.0 / total)
    row, col = grid()
    diagonal = jnp.where(row == col, (hi[:N, :N] - share) + lo[:N, :N], 0.0)
    mixed_hi = jnp.where(row < col, hi[:N, :N], hi[N:, N:])
    mixed_lo = put_diagonal(jnp.where(row < col, lo[:N, :N], lo[N:, N:]), diagonal)
    out_ref[: 2 * TILES] = pack(mixed_hi, mixed_lo)
    out_ref[2 * TILES :] = pack(hi[:N, N:], lo[:N, N:])


def local_products(snapshots, basis, devices):
    rows = snapshots.shape[0]
    total = rows * devices
    return pl.pallas_call(
        functools.partial(local_kernel, 1.0 / devices, total),
        out_shape=jax.ShapeDtypeStruct((4 * TILES, TILE, N), F32),
        in_specs=[pl.BlockSpec(memory_space=pltpu.HBM)] * 2,
        scratch_shapes=[pltpu.VMEM((rows, 2 * N), F32), pltpu.SemaphoreType.DMA((2,))],
        compiler_params=pltpu.CompilerParams(vmem_limit_bytes=32 << 20),
    )(snapshots, basis)


def sum_kernel(in_ref, out_ref):
    parts = [(in_ref[i], None) for i in range(in_ref.shape[0])]
    while len(parts) > 1:
        added = []
        for (a, a_left), (b, b_left) in zip(parts[::2], parts[1::2]):
            s, left = two_sum(a, b)
            if a_left is not None:
                left = left + (a_left + b_left)
            added.append((s, left))
        parts = added
    s, left = parts[0]
    lower = lax.broadcasted_iota(jnp.int32, s.shape, 0) >= TILE // 2
    s = s + jnp.where(lower, pltpu.roll(left, TILE // 2, 0), 0.0)
    for i in range(out_ref.shape[0]):
        out_ref[i] = s


def sum_and_copy(parts, copies):
    return pl.pallas_call(
        sum_kernel,
        out_shape=jax.ShapeDtypeStruct((copies, TILE, N), F32),
        compiler_params=pltpu.CompilerParams(vmem_limit_bytes=32 << 20),
    )(parts)


def factor_inverse(gram):
    sub = lax.broadcasted_iota(jnp.int32, (TILE, N), 0)
    lane = lax.broadcasted_iota(jnp.int32, (TILE, N), 1)
    work = gram
    inv = jnp.where(
        lax.broadcasted_iota(jnp.int32, (N, N), 0)
        == lax.broadcasted_iota(jnp.int32, (N, N), 1),
        1.0,
        0.0,
    ).astype(F32)
    upper_rows, inv_rows = [], []
    for p in range(TILES):
        at = p * TILE
        rows = work[:TILE, :]
        irow = inv[:TILE, :]
        d = {}
        for j in range(TILE):
            col = jnp.broadcast_to(rows[:, at + j : at + j + 1], (TILE, N))
            for i in range(j + 1):
                d[i, j] = jnp.broadcast_to(col[i : i + 1, :], (TILE, N))
        r = []
        for k in range(TILE):
            piv = d[k, k]
            y = lax.rsqrt(piv)
            y = y * (1.5 - 0.5 * piv * y * y)
            r.append(y)
            for j in range(k + 1, TILE):
                d[k, j] = d[k, j] * y
            for i in range(k + 1, TILE):
                for j in range(i, TILE):
                    d[i, j] = d[i, j] - d[k, i] * d[k, j]
        li = {}
        for j in range(TILE):
            li[j, j] = r[j]
            for i in range(j + 1, TILE):
                acc = d[j, i] * li[j, j]
                for k in range(j + 1, i):
                    acc = acc + d[k, i] * li[k, j]
                li[i, j] = -(acc * r[i])
        new_u = jnp.zeros((TILE, N), F32)
        new_i = jnp.zeros((TILE, N), F32)
        for k in range(TILE):
            colk = jnp.zeros((TILE, N), F32)
            for i in range(k, TILE):
                colk = jnp.where(sub == i, li[i, k], colk)
            new_u = new_u + colk * jnp.broadcast_to(rows[k : k + 1, :], (TILE, N))
            new_i = new_i + colk * jnp.broadcast_to(irow[k : k + 1, :], (TILE, N))
        new_u = jnp.where(lane >= at + sub, new_u, 0.0)
        upper_rows.append(new_u)
        inv_rows.append(new_i)
        if p + 1 < TILES:
            both = jnp.concatenate([new_u, new_i], axis=1)
            b1 = both.astype(BF16)
            rest = both - b1.astype(F32)
            b2 = rest.astype(BF16)
            b3 = (rest - b2.astype(F32)).astype(BF16)
            f1, f2, f3 = b1.astype(F32), b2.astype(F32), b3.astype(F32)
            left = jnp.concatenate([f[:, :N] for f in (f1, f1, f2, f1, f2, f3)], axis=0)
            right = jnp.concatenate([f1, f2, f1, f3, f2, f1], axis=0).astype(BF16)
            left = left.T.astype(BF16)[at + TILE :, :]
            upd = dot(left, right)
            work = work[TILE:, :] - upd[:, :N]
            inv = inv[TILE:, :] - upd[:, N:]
    return jnp.concatenate(upper_rows, axis=0), jnp.concatenate(inv_rows, axis=0)


def three_dot_t(left, right):
    l1, r1 = left.astype(BF16), right.astype(BF16)
    l2 = (left - l1.astype(F32)).astype(BF16)
    r2 = (right - r1.astype(F32)).astype(BF16)
    return dot_t(jnp.concatenate([l1, l1, l2], 0), jnp.concatenate([r1, r2, r1], 0))


def three_dot(left, right):
    l1, r1 = left.astype(BF16), right.astype(BF16)
    l2 = (left - l1.astype(F32)).astype(BF16)
    r2 = (right - r1.astype(F32)).astype(BF16)
    return dot(jnp.concatenate([l1, l1, l2], 1), jnp.concatenate([r1, r2, r1], 0))


NEAR = 2.0**-4
TURNS = 4


def near_factor(off):
    row, col = grid()
    weight = jnp.where(row < col, 1.0, jnp.where(row == col, 0.5, 0.0))
    n = off * weight
    for _ in range(TURNS):
        n = (off - three_dot_t(n, n)) * weight
    eye = jnp.where(row == col, 1.0, 0.0)
    n2 = three_dot(n, n)
    n4 = three_dot(n2, n2)
    inverse = (eye - n) + (n2 - three_dot(n, n2))
    inverse = inverse + three_dot(inverse, n4)
    return eye + n, inverse


def final_kernel(sums_ref, snap_ref, basis_ref, modes_ref, factor_ref, coef_ref, u_ref, i_ref):
    row, col = grid()
    mixed_hi, mixed_lo = unpack(sums_ref[: 2 * TILES])
    cross = unpack(sums_ref[2 * TILES :])
    diagonal, mixed_lo = take_diagonal(mixed_lo)
    turned_hi, turned_lo = mixed_hi.T, mixed_lo.T
    one = jnp.where(row == col, 1.0, 0.0)
    one_hi, one_lo = two_sum(one, diagonal)
    basis_gram = (
        jnp.where(row == col, one_hi, jnp.where(row < col, mixed_hi, turned_hi)),
        jnp.where(row == col, one_lo, jnp.where(row < col, mixed_lo, turned_lo)),
    )
    snap_gram = (
        jnp.where(row < col, turned_hi, mixed_hi),
        jnp.where(row < col, turned_lo, mixed_lo),
    )
    coef_two = cross[0] - dot(basis_gram[0], cross[0], HIGHEST)
    coef = cross[0] + coef_two
    coef_ref[...] = coef
    second = snap_ref[...] - dot(basis_ref[...], coef, HIGHEST)

    g_c = exact_dot(slices(*basis_gram, 1, 5, 16), slices(coef, None, 0, 5, 16))
    held = pair_sum((2.0 * cross[0], 2.0 * cross[1]), (-g_c[0], -g_c[1]))
    held = normal(held)
    c_h = exact_dot(slices(coef.T, None, 1, 5, 16), slices(*held, 0, 5, 16))
    c_h = pair_sum((0.5 * c_h[0], 0.5 * c_h[1]), (0.5 * c_h[0].T, 0.5 * c_h[1].T))
    gram_one = normal(pair_sum(snap_gram, (-c_h[0], -c_h[1])))

    upper_one, inv_one_t = factor_inverse(gram_one[0])
    inv_one = inv_one_t.T
    g_i = exact_dot(slices(*gram_one, 1, 5, 16), slices(inv_one, None, 0, 5, 16))
    g_i = normal(g_i)
    i_g_i = exact_dot(slices(inv_one_t, None, 1, 5, 16), slices(*g_i, 0, 5, 16))
    off = (i_g_i[0] - one) + i_g_i[1]
    is_near = jnp.sum(off * off) <= NEAR * NEAR

    @pl.when(is_near)
    def _():
        u_ref[...], i_ref[...] = near_factor(off)

    @pl.when(jnp.logical_not(is_near))
    def _():
        upper, inv_t = factor_inverse(one + off)
        u_ref[...] = upper
        i_ref[...] = inv_t.T

    factor_ref[...] = dot(u_ref[...], upper_one, HIGHEST)
    both = dot(inv_one, i_ref[...], HIGHEST)
    modes_ref[...] = dot(second, both, HIGHEST)


def finish(sums, snapshots, basis):
    rows = snapshots.shape[0]
    return pl.pallas_call(
        final_kernel,
        out_shape=(
            jax.ShapeDtypeStruct((rows, N), F32),
            jax.ShapeDtypeStruct((N, N), F32),
            jax.ShapeDtypeStruct((N, N), F32),
        ),
        scratch_shapes=[pltpu.VMEM((N, N), F32)] * 2,
        compiler_params=pltpu.CompilerParams(vmem_limit_bytes=48 << 20),
    )(sums, snapshots, basis)


def body(snapshots, basis):
    group, many = lax.axis_size("grp"), lax.axis_size("dev")
    local = local_products(snapshots, basis, group * many)
    parts = lax.all_to_all(local, "dev", 0, 0)
    mine = sum_and_copy(parts, group)
    parts = lax.all_to_all(mine, "grp", 0, 0)
    mine = sum_and_copy(parts, many)
    sums = lax.all_to_all(mine, "dev", 0, 0)
    return finish(sums, snapshots, basis)


def solution(mesh):
    return jax.shard_map(
        body,
        mesh=mesh,
        in_specs=(P(("grp", "dev"), None), P(("grp", "dev"), None)),
        out_specs=(P(("grp", "dev"), None), P(), P()),
        check_vma=False,
    )
```

```python
import functools

import jax
import jax.numpy as jnp
from jax import lax
from jax.experimental import pallas as pl
from jax.experimental.pallas import tpu as pltpu
from jax.sharding import PartitionSpec as P

HIGHEST = lax.Precision.HIGHEST
F32, BF16 = jnp.float32, jnp.bfloat16
N = 128
TILE = 8
TILES = N // TILE


def two_sum(a, b):
    s = a + b
    t = s - a
    return s, (a - (s - t)) + (b - t)


def pair_sum(a, b):
    s, e = two_sum(a[0], b[0])
    return s, e + (a[1] + b[1])


def normal(a):
    s = a[0] + a[1]
    return s, a[1] - (s - a[0])


def dot_t(a, b, precision=None):
    return lax.dot_general(
        a, b, (((0,), (0,)), ((), ())), precision=precision, preferred_element_type=F32
    )


def dot(a, b, precision=None):
    return jnp.dot(a, b, precision=precision, preferred_element_type=F32)


def slices(hi, lo, axis, count, shift):
    step = jnp.max(jnp.abs(hi), axis=axis, keepdims=True) * (2.0**shift)
    first = (hi + step) - step
    rest = hi - first
    step = step * 2.0**-8
    second = (rest + step) - step
    rest = rest - second
    if lo is not None:
        rest = rest + lo
    out = [first.astype(BF16), second.astype(BF16)]
    while len(out) < count:
        part = rest.astype(BF16)
        rest = rest - part.astype(F32)
        out.append(part)
    return out


def exact_dot(left, right):
    wide = jnp.concatenate(left, axis=1)
    tall = jnp.concatenate(right[::-1], axis=0)
    n = len(left)
    terms = [dot(wide[:, : N * k], tall[N * (n - k) :, :]) for k in range(1, n + 1)]
    low = terms[-1]
    for t in terms[-2:1:-1]:
        low = low + t
    s, e = two_sum(terms[0], terms[1])
    return s, e + low


def grid(rows=N):
    return (
        lax.broadcasted_iota(jnp.int32, (rows, N), 0),
        lax.broadcasted_iota(jnp.int32, (rows, N), 1),
    )


def put_diagonal(rest, diagonal):
    row, col = grid(N // 2)
    near = pltpu.roll(diagonal[N // 2 :, :], N - N // 4, 1)
    far = pltpu.roll(diagonal[: N // 2, :], N // 2, 1)
    top = jnp.where(col == row + N // 4, near, rest[: N // 2, :])
    top = jnp.where(col == row + N // 2, far, top)
    return jnp.concatenate([top, rest[N // 2 :, :]], axis=0)


def take_diagonal(rest):
    row, col = grid(N // 2)
    top = rest[: N // 2, :]
    near, far = col == row + N // 4, col == row + N // 2
    first = pltpu.roll(jnp.where(far, top, 0.0), N // 2, 1)
    last = pltpu.roll(jnp.where(near, top, 0.0), N // 4, 1)
    top = jnp.where(near | far, 0.0, top)
    return (
        jnp.concatenate([first, last], axis=0),
        jnp.concatenate([top, rest[N // 2 :, :]], axis=0),
    )


def pack(hi, lo):
    hi, lo = hi.reshape(TILES, TILE, N), lo.reshape(TILES, TILE, N)
    upper = lax.broadcasted_iota(jnp.int32, hi.shape, 1) < TILE // 2
    even = jnp.where(upper, hi, pltpu.roll(lo, TILE // 2, 1))
    odd = jnp.where(upper, pltpu.roll(hi, TILE // 2, 1), lo)
    return jnp.stack([even, odd], axis=1).reshape(2 * TILES, TILE, N)


def unpack(pieces):
    pieces = pieces.reshape(TILES, 2, TILE, N)
    even, odd = pieces[:, 0], pieces[:, 1]
    upper = lax.broadcasted_iota(jnp.int32, even.shape, 1) < TILE // 2
    hi = jnp.where(upper, even, pltpu.roll(odd, TILE // 2, 1))
    lo = jnp.where(upper, pltpu.roll(even, TILE // 2, 1), odd)
    return hi.reshape(N, N), lo.reshape(N, N)


def local_kernel(share, total, snap_hbm, basis_hbm, out_ref, z_ref, sem):
    copies = [
        pltpu.make_async_copy(basis_hbm, z_ref.at[:, :N], sem.at[0]),
        pltpu.make_async_copy(snap_hbm, z_ref.at[:, N:], sem.at[1]),
    ]
    for copy in copies:
        copy.start()
    for copy in copies:
        copy.wait()
    a, b, c, d = slices(z_ref[...], None, 0, 4, 17)
    main = dot_t(a, a)
    low_1 = dot_t(a, b)
    low_2 = dot_t(a, c) + 0.5 * dot_t(b, b)
    low_3 = dot_t(a, d) + dot_t(b, c)
    low_4 = dot_t(b, d) + 0.5 * dot_t(c, c)
    half = low_1 + (low_2 + (low_3 + low_4))
    hi, lo = two_sum(main, half + half.T)
    hi, lo = hi * (1.0 / total), lo * (1.0 / total)
    row, col = grid()
    diagonal = jnp.where(row == col, (hi[:N, :N] - share) + lo[:N, :N], 0.0)
    mixed_hi = jnp.where(row < col, hi[:N, :N], hi[N:, N:])
    mixed_lo = put_diagonal(jnp.where(row < col, lo[:N, :N], lo[N:, N:]), diagonal)
    out_ref[: 2 * TILES] = pack(mixed_hi, mixed_lo)
    out_ref[2 * TILES :] = pack(hi[:N, N:], lo[:N, N:])


def local_products(snapshots, basis, devices):
    rows = snapshots.shape[0]
    total = rows * devices
    return pl.pallas_call(
        functools.partial(local_kernel, 1.0 / devices, total),
        out_shape=jax.ShapeDtypeStruct((4 * TILES, TILE, N), F32),
        in_specs=[pl.BlockSpec(memory_space=pltpu.HBM)] * 2,
        scratch_shapes=[pltpu.VMEM((rows, 2 * N), F32), pltpu.SemaphoreType.DMA((2,))],
        compiler_params=pltpu.CompilerParams(vmem_limit_bytes=32 << 20),
    )(snapshots, basis)


def sum_kernel(in_ref, out_ref):
    parts = [(in_ref[i], None) for i in range(in_ref.shape[0])]
    while len(parts) > 1:
        added = []
        for (a, a_left), (b, b_left) in zip(parts[::2], parts[1::2]):
            s, left = two_sum(a, b)
            if a_left is not None:
                left = left + (a_left + b_left)
            added.append((s, left))
        parts = added
    s, left = parts[0]
    lower = lax.broadcasted_iota(jnp.int32, s.shape, 0) >= TILE // 2
    s = s + jnp.where(lower, pltpu.roll(left, TILE // 2, 0), 0.0)
    for i in range(out_ref.shape[0]):
        out_ref[i] = s


def sum_and_copy(parts, copies):
    return pl.pallas_call(
        sum_kernel,
        out_shape=jax.ShapeDtypeStruct((copies, TILE, N), F32),
        compiler_params=pltpu.CompilerParams(vmem_limit_bytes=32 << 20),
    )(parts)


def spread_row(tile, k):
    return jnp.broadcast_to(tile[k : k + 1, :], (TILE, N))


def spread_lane(tile, j):
    return jnp.broadcast_to(tile[:, j : j + 1], (TILE, N))


def factor_inverse(gram):
    sub = lax.broadcasted_iota(jnp.int32, (TILE, N), 0)
    lane = lax.broadcasted_iota(jnp.int32, (TILE, N), 1)
    work = [gram[q * TILE : (q + 1) * TILE, :] for q in range(TILES)]
    upper, inverse = [], []
    for p in range(TILES):
        at, after = p * TILE, range(p + 1, TILES)
        d = {}
        for j in range(TILE):
            column = spread_lane(work[p], at + j)
            for i in range(j + 1):
                d[i, j] = spread_row(column, i)
        below = {(q, j): spread_lane(work[q], at + j) for q in after for j in range(TILE)}
        right = lane >= at + TILE
        block = (lane >= at) & (lane < at + TILE)
        for q in after:
            work[q] = jnp.where(block, 0.0, work[q])
        left = jnp.where(lane < at, work[p], jnp.where(lane == at + sub, 1.0, 0.0))
        rows = [(spread_row(work[p], k), spread_row(left, k)) for k in range(TILE)]
        new = [jnp.zeros((TILE, N), F32)] * 2
        for k in range(TILE):
            scale = lax.rsqrt(d[k, k])
            for j in range(k + 1, TILE):
                d[k, j] = d[k, j] * scale
            for i in range(k + 1, TILE):
                for j in range(i, TILE):
                    d[i, j] = d[i, j] - d[k, i] * d[k, j]
            row = (rows[k][0] * scale, rows[k][1] * scale)
            for i in range(k + 1, TILE):
                rows[i] = tuple(a - d[k, i] * b for a, b in zip(rows[i], row))
            finished = jnp.where(right, *row)
            for q in after:
                m = below[q, k] * scale
                for j in range(k + 1, TILE):
                    below[q, j] = below[q, j] - m * d[k, j]
                work[q] = work[q] - m * finished
            new = [jnp.where(sub == k, a, b) for a, b in zip(row, new)]
        upper.append(jnp.where(lane >= at + sub, new[0], 0.0))
        inverse.append(jnp.where(right, 0.0, new[1]))
    return jnp.concatenate(upper, axis=0), jnp.concatenate(inverse, axis=0)


def three_dot_t(left, right):
    l1, r1 = left.astype(BF16), right.astype(BF16)
    l2 = (left - l1.astype(F32)).astype(BF16)
    r2 = (right - r1.astype(F32)).astype(BF16)
    return dot_t(jnp.concatenate([l1, l1, l2], 0), jnp.concatenate([r1, r2, r1], 0))


def three_dot(left, right):
    l1, r1 = left.astype(BF16), right.astype(BF16)
    l2 = (left - l1.astype(F32)).astype(BF16)
    r2 = (right - r1.astype(F32)).astype(BF16)
    return dot(jnp.concatenate([l1, l1, l2], 1), jnp.concatenate([r1, r2, r1], 0))


NEAR = 2.0**-4
TURNS = 4


def near_factor(off):
    row, col = grid()
    weight = jnp.where(row < col, 1.0, jnp.where(row == col, 0.5, 0.0))
    n = off * weight
    for _ in range(TURNS):
        n = (off - three_dot_t(n, n)) * weight
    eye = jnp.where(row == col, 1.0, 0.0)
    n2 = three_dot(n, n)
    n4 = three_dot(n2, n2)
    inverse = (eye - n) + (n2 - three_dot(n, n2))
    inverse = inverse + three_dot(inverse, n4)
    return eye + n, inverse


def final_kernel(sums_ref, snap_ref, basis_ref, modes_ref, factor_ref, coef_ref, u_ref, i_ref):
    row, col = grid()
    mixed_hi, mixed_lo = unpack(sums_ref[: 2 * TILES])
    cross = unpack(sums_ref[2 * TILES :])
    diagonal, mixed_lo = take_diagonal(mixed_lo)
    turned_hi, turned_lo = mixed_hi.T, mixed_lo.T
    one = jnp.where(row == col, 1.0, 0.0)
    one_hi, one_lo = two_sum(one, diagonal)
    basis_gram = (
        jnp.where(row == col, one_hi, jnp.where(row < col, mixed_hi, turned_hi)),
        jnp.where(row == col, one_lo, jnp.where(row < col, mixed_lo, turned_lo)),
    )
    snap_gram = (
        jnp.where(row < col, turned_hi, mixed_hi),
        jnp.where(row < col, turned_lo, mixed_lo),
    )
    coef_two = cross[0] - dot(basis_gram[0], cross[0], HIGHEST)
    coef = cross[0] + coef_two
    coef_ref[...] = coef
    second = snap_ref[...] - dot(basis_ref[...], coef, HIGHEST)

    g_c = exact_dot(slices(*basis_gram, 1, 5, 16), slices(coef, None, 0, 5, 16))
    held = pair_sum((2.0 * cross[0], 2.0 * cross[1]), (-g_c[0], -g_c[1]))
    held = normal(held)
    c_h = exact_dot(slices(coef.T, None, 1, 5, 16), slices(*held, 0, 5, 16))
    c_h = pair_sum((0.5 * c_h[0], 0.5 * c_h[1]), (0.5 * c_h[0].T, 0.5 * c_h[1].T))
    gram_one = normal(pair_sum(snap_gram, (-c_h[0], -c_h[1])))

    upper_one, inv_one_t = factor_inverse(gram_one[0])
    inv_one = inv_one_t.T
    g_i = exact_dot(slices(*gram_one, 1, 5, 16), slices(inv_one, None, 0, 5, 16))
    g_i = normal(g_i)
    i_g_i = exact_dot(slices(inv_one_t, None, 1, 5, 16), slices(*g_i, 0, 5, 16))
    off = (i_g_i[0] - one) + i_g_i[1]
    is_near = jnp.sum(off * off) <= NEAR * NEAR

    @pl.when(is_near)
    def _():
        u_ref[...], i_ref[...] = near_factor(off)

    @pl.when(jnp.logical_not(is_near))
    def _():
        upper, inv_t = factor_inverse(one + off)
        u_ref[...] = upper
        i_ref[...] = inv_t.T

    factor_ref[...] = dot(u_ref[...], upper_one, HIGHEST)
    both = dot(inv_one, i_ref[...], HIGHEST)
    modes_ref[...] = dot(second, both, HIGHEST)


def finish(sums, snapshots, basis):
    rows = snapshots.shape[0]
    return pl.pallas_call(
        final_kernel,
        out_shape=(
            jax.ShapeDtypeStruct((rows, N), F32),
            jax.ShapeDtypeStruct((N, N), F32),
            jax.ShapeDtypeStruct((N, N), F32),
        ),
        scratch_shapes=[pltpu.VMEM((N, N), F32)] * 2,
        compiler_params=pltpu.CompilerParams(vmem_limit_bytes=48 << 20),
    )(sums, snapshots, basis)


def body(snapshots, basis):
    group, many = lax.axis_size("grp"), lax.axis_size("dev")
    local = local_products(snapshots, basis, group * many)
    parts = lax.all_to_all(local, "dev", 0, 0)
    mine = sum_and_copy(parts, group)
    parts = lax.all_to_all(mine, "grp", 0, 0)
    mine = sum_and_copy(parts, many)
    sums = lax.all_to_all(mine, "dev", 0, 0)
    return finish(sums, snapshots, basis)


def solution(mesh):
    return jax.shard_map(
        body,
        mesh=mesh,
        in_specs=(P(("grp", "dev"), None), P(("grp", "dev"), None)),
        out_specs=(P(("grp", "dev"), None), P(), P()),
        check_vma=False,
    )
```

```python
import functools

import jax
import jax.numpy as jnp
from jax import lax
from jax.experimental import pallas as pl
from jax.experimental.pallas import tpu as pltpu
from jax.sharding import Mesh
from jax.sharding import PartitionSpec as P

HIGHEST = lax.Precision.HIGHEST
F32, BF16 = jnp.float32, jnp.bfloat16
N = 128
TILE = 8
TILES = N // TILE


def two_sum(a, b):
    s = a + b
    t = s - a
    return s, (a - (s - t)) + (b - t)


def pair_sum(a, b):
    s, e = two_sum(a[0], b[0])
    return s, e + (a[1] + b[1])


def normal(a):
    s = a[0] + a[1]
    return s, a[1] - (s - a[0])


def dot_t(a, b, precision=None):
    return lax.dot_general(
        a, b, (((0,), (0,)), ((), ())), precision=precision, preferred_element_type=F32
    )


def dot(a, b, precision=None):
    return jnp.dot(a, b, precision=precision, preferred_element_type=F32)


def slices(hi, lo, axis, count, shift):
    step = jnp.max(jnp.abs(hi), axis=axis, keepdims=True) * (2.0**shift)
    first = (hi + step) - step
    rest = hi - first
    step = step * 2.0**-8
    second = (rest + step) - step
    rest = rest - second
    if lo is not None:
        rest = rest + lo
    out = [first.astype(BF16), second.astype(BF16)]
    while len(out) < count:
        part = rest.astype(BF16)
        rest = rest - part.astype(F32)
        out.append(part)
    return out


def exact_dot(left, right):
    wide = jnp.concatenate(left, axis=1)
    tall = jnp.concatenate(right[::-1], axis=0)
    n = len(left)
    terms = [dot(wide[:, : N * k], tall[N * (n - k) :, :]) for k in range(1, n + 1)]
    low = terms[-1]
    for t in terms[-2:1:-1]:
        low = low + t
    s, e = two_sum(terms[0], terms[1])
    return s, e + low


def grid(rows=N):
    return (
        lax.broadcasted_iota(jnp.int32, (rows, N), 0),
        lax.broadcasted_iota(jnp.int32, (rows, N), 1),
    )


def put_diagonal(rest, diagonal):
    row, col = grid(N // 2)
    near = pltpu.roll(diagonal[N // 2 :, :], N - N // 4, 1)
    far = pltpu.roll(diagonal[: N // 2, :], N // 2, 1)
    top = jnp.where(col == row + N // 4, near, rest[: N // 2, :])
    top = jnp.where(col == row + N // 2, far, top)
    return jnp.concatenate([top, rest[N // 2 :, :]], axis=0)


def take_diagonal(rest):
    row, col = grid(N // 2)
    top = rest[: N // 2, :]
    near, far = col == row + N // 4, col == row + N // 2
    first = pltpu.roll(jnp.where(far, top, 0.0), N // 2, 1)
    last = pltpu.roll(jnp.where(near, top, 0.0), N // 4, 1)
    top = jnp.where(near | far, 0.0, top)
    return (
        jnp.concatenate([first, last], axis=0),
        jnp.concatenate([top, rest[N // 2 :, :]], axis=0),
    )


def pack(hi, lo):
    hi, lo = hi.reshape(TILES, TILE, N), lo.reshape(TILES, TILE, N)
    upper = lax.broadcasted_iota(jnp.int32, hi.shape, 1) < TILE // 2
    even = jnp.where(upper, hi, pltpu.roll(lo, TILE // 2, 1))
    odd = jnp.where(upper, pltpu.roll(hi, TILE // 2, 1), lo)
    return jnp.stack([even, odd], axis=1).reshape(2 * TILES, TILE, N)


def unpack(even, odd):
    upper = lax.broadcasted_iota(jnp.int32, even.shape, 1) < TILE // 2
    hi = jnp.where(upper, even, pltpu.roll(odd, TILE // 2, 1))
    lo = jnp.where(upper, pltpu.roll(even, TILE // 2, 1), odd)
    return hi.reshape(N, N), lo.reshape(N, N)


def local_kernel(share, total, snap_hbm, basis_hbm, out_ref, z_ref, sem):
    copies = [
        pltpu.make_async_copy(basis_hbm, z_ref.at[:, :N], sem.at[0]),
        pltpu.make_async_copy(snap_hbm, z_ref.at[:, N:], sem.at[1]),
    ]
    for copy in copies:
        copy.start()
    for copy in copies:
        copy.wait()
    a, b, c, d = slices(z_ref[...], None, 0, 4, 17)
    main = dot_t(a, a)
    low_1 = dot_t(a, b)
    low_2 = dot_t(a, c) + 0.5 * dot_t(b, b)
    low_3 = dot_t(a, d) + dot_t(b, c)
    low_4 = dot_t(b, d) + 0.5 * dot_t(c, c)
    half = low_1 + (low_2 + (low_3 + low_4))
    hi, lo = two_sum(main, half + half.T)
    hi, lo = hi * (1.0 / total), lo * (1.0 / total)
    row, col = grid()
    diagonal = jnp.where(row == col, (hi[:N, :N] - share) + lo[:N, :N], 0.0)
    mixed_hi = jnp.where(row < col, hi[:N, :N], hi[N:, N:])
    mixed_lo = put_diagonal(jnp.where(row < col, lo[:N, :N], lo[N:, N:]), diagonal)
    out_ref[: 2 * TILES] = pack(mixed_hi, mixed_lo)
    out_ref[2 * TILES :] = pack(hi[:N, N:], lo[:N, N:])


def local_products(snapshots, basis, devices):
    rows = snapshots.shape[0]
    total = rows * devices
    return pl.pallas_call(
        functools.partial(local_kernel, 1.0 / devices, total),
        out_shape=jax.ShapeDtypeStruct((4 * TILES, TILE, N), F32),
        in_specs=[pl.BlockSpec(memory_space=pltpu.HBM)] * 2,
        scratch_shapes=[pltpu.VMEM((rows, 2 * N), F32), pltpu.SemaphoreType.DMA((2,))],
        compiler_params=pltpu.CompilerParams(vmem_limit_bytes=32 << 20),
    )(snapshots, basis)


def sum_kernel(in_ref, out_ref):
    parts = [(in_ref[i], None) for i in range(in_ref.shape[0])]
    while len(parts) > 1:
        added = []
        for (a, a_left), (b, b_left) in zip(parts[::2], parts[1::2]):
            s, left = two_sum(a, b)
            if a_left is not None:
                left = left + (a_left + b_left)
            added.append((s, left))
        parts = added
    s, left = parts[0]
    lower = lax.broadcasted_iota(jnp.int32, s.shape, 0) >= TILE // 2
    s = s + jnp.where(lower, pltpu.roll(left, TILE // 2, 0), 0.0)
    for i in range(out_ref.shape[0]):
        out_ref[i] = s


def sum_and_copy(parts, copies):
    return pl.pallas_call(
        sum_kernel,
        out_shape=jax.ShapeDtypeStruct((copies, TILE, N), F32),
        compiler_params=pltpu.CompilerParams(vmem_limit_bytes=32 << 20),
    )(parts)


def spread_row(tile, k):
    return jnp.broadcast_to(tile[k : k + 1, :], (TILE, N))


def spread_lane(tile, j):
    return jnp.broadcast_to(tile[:, j : j + 1], (TILE, N))


def factor_inverse(gram):
    sub = lax.broadcasted_iota(jnp.int32, (TILE, N), 0)
    lane = lax.broadcasted_iota(jnp.int32, (TILE, N), 1)
    work = [gram[q * TILE : (q + 1) * TILE, :] for q in range(TILES)]
    upper, inverse = [], []
    for p in range(TILES):
        at, after = p * TILE, range(p + 1, TILES)
        d = {}
        for j in range(TILE):
            column = spread_lane(work[p], at + j)
            for i in range(j + 1):
                d[i, j] = spread_row(column, i)
        below = {(q, j): spread_lane(work[q], at + j) for q in after for j in range(TILE)}
        right = lane >= at + TILE
        block = (lane >= at) & (lane < at + TILE)
        for q in after:
            work[q] = jnp.where(block, 0.0, work[q])
        left = jnp.where(lane < at, work[p], jnp.where(lane == at + sub, 1.0, 0.0))
        rows = [(spread_row(work[p], k), spread_row(left, k)) for k in range(TILE)]
        new = [jnp.zeros((TILE, N), F32)] * 2
        for k in range(TILE):
            scale = lax.rsqrt(d[k, k])
            for j in range(k + 1, TILE):
                d[k, j] = d[k, j] * scale
            for i in range(k + 1, TILE):
                for j in range(i, TILE):
                    d[i, j] = d[i, j] - d[k, i] * d[k, j]
            row = (rows[k][0] * scale, rows[k][1] * scale)
            for i in range(k + 1, TILE):
                rows[i] = tuple(a - d[k, i] * b for a, b in zip(rows[i], row))
            finished = jnp.where(right, *row)
            for q in after:
                m = below[q, k] * scale
                for j in range(k + 1, TILE):
                    below[q, j] = below[q, j] - m * d[k, j]
                work[q] = work[q] - m * finished
            new = [jnp.where(sub == k, a, b) for a, b in zip(row, new)]
        upper.append(jnp.where(lane >= at + sub, new[0], 0.0))
        inverse.append(jnp.where(right, 0.0, new[1]))
    return jnp.concatenate(upper, axis=0), jnp.concatenate(inverse, axis=0)


def three_dot_t(left, right):
    l1, r1 = left.astype(BF16), right.astype(BF16)
    l2 = (left - l1.astype(F32)).astype(BF16)
    r2 = (right - r1.astype(F32)).astype(BF16)
    return dot_t(jnp.concatenate([l1, l1, l2], 0), jnp.concatenate([r1, r2, r1], 0))


def three_dot(left, right):
    l1, r1 = left.astype(BF16), right.astype(BF16)
    l2 = (left - l1.astype(F32)).astype(BF16)
    r2 = (right - r1.astype(F32)).astype(BF16)
    return dot(jnp.concatenate([l1, l1, l2], 1), jnp.concatenate([r1, r2, r1], 0))


NEAR = 2.0**-4
TURNS = 4


def near_factor(off, inv_one):
    row, col = grid()
    weight = jnp.where(row < col, 1.0, jnp.where(row == col, 0.5, 0.0))
    n = off * weight
    for _ in range(TURNS):
        n = (off - three_dot_t(n, n)) * weight
    first = inv_one - dot(inv_one, n, HIGHEST)
    n2 = three_dot(n, n)
    n2 = n2 + three_dot(n2, n2)
    return jnp.where(row == col, 1.0, 0.0) + n, first + three_dot(first, n2)


PARTS = 4


def final_kernel(own_ref, other_ref, snap_ref, basis_ref, modes_hbm, factor_hbm, coef_hbm,
                 modes_ref, factor_ref, coef_ref, u_ref, t_ref, sem):
    row, col = grid()
    own, other = own_ref[...], other_ref[...]
    is_first = lax.axis_index("core") == 0
    even, odd = jnp.where(is_first, own, other), jnp.where(is_first, other, own)
    mixed_hi, mixed_lo = unpack(even[:TILES], odd[:TILES])
    cross = unpack(even[TILES:], odd[TILES:])
    diagonal, mixed_lo = take_diagonal(mixed_lo)
    turned_hi, turned_lo = mixed_hi.T, mixed_lo.T
    one = jnp.where(row == col, 1.0, 0.0)
    one_hi, one_lo = two_sum(one, diagonal)
    basis_gram = (
        jnp.where(row == col, one_hi, jnp.where(row < col, mixed_hi, turned_hi)),
        jnp.where(row == col, one_lo, jnp.where(row < col, mixed_lo, turned_lo)),
    )
    snap_gram = (
        jnp.where(row < col, turned_hi, mixed_hi),
        jnp.where(row < col, turned_lo, mixed_lo),
    )
    coef_two = cross[0] - dot(basis_gram[0], cross[0], HIGHEST)
    coef = cross[0] + coef_two
    coef_ref[...] = coef
    coef_copy = pltpu.make_async_copy(coef_ref, coef_hbm, sem.at[0])
    coef_copy.start()
    second = snap_ref[...] - dot(basis_ref[...], coef, HIGHEST)

    g_c = exact_dot(slices(*basis_gram, 1, 5, 16), slices(coef, None, 0, 5, 16))
    held = pair_sum((2.0 * cross[0], 2.0 * cross[1]), (-g_c[0], -g_c[1]))
    held = normal(held)
    c_h = exact_dot(slices(coef.T, None, 1, 5, 16), slices(*held, 0, 5, 16))
    c_h = pair_sum((0.5 * c_h[0], 0.5 * c_h[1]), (0.5 * c_h[0].T, 0.5 * c_h[1].T))
    gram_one = normal(pair_sum(snap_gram, (-c_h[0], -c_h[1])))

    upper_one, inv_one_t = factor_inverse(gram_one[0])
    inv_one = inv_one_t.T
    g_i = exact_dot(slices(*gram_one, 1, 5, 16), slices(inv_one, None, 0, 5, 16))
    g_i = normal(g_i)
    i_g_i = exact_dot(slices(inv_one_t, None, 1, 5, 16), slices(*g_i, 0, 5, 16))
    off = (i_g_i[0] - one) + i_g_i[1]
    is_near = jnp.sum(off * off) <= NEAR * NEAR

    u_ref[...], t_ref[...] = near_factor(off, inv_one)

    @pl.when(jnp.logical_not(is_near))
    def _():
        upper, inv_t = factor_inverse(one + off)
        u_ref[...] = upper
        t_ref[...] = dot(inv_one, inv_t.T, HIGHEST)

    both = t_ref[...]
    copies = [coef_copy]
    step = modes_ref.shape[0] // PARTS
    for i in range(PARTS):
        part = slice(i * step, (i + 1) * step)
        modes_ref[part, :] = dot(second[part, :], both, HIGHEST)
        copies.append(
            pltpu.make_async_copy(modes_ref.at[part, :], modes_hbm.at[part, :], sem.at[2 + i])
        )
        copies[-1].start()
        if i == 0:
            factor_ref[...] = dot(u_ref[...], upper_one, HIGHEST)
            copies.append(pltpu.make_async_copy(factor_ref, factor_hbm, sem.at[1]))
            copies[-1].start()
    for copy in copies:
        copy.wait()


def finish(own, other, snapshots, basis):
    rows = snapshots.shape[0]
    square = pltpu.VMEM((N, N), F32)
    return pl.pallas_call(
        final_kernel,
        out_shape=(
            jax.ShapeDtypeStruct((rows, N), F32),
            jax.ShapeDtypeStruct((N, N), F32),
            jax.ShapeDtypeStruct((N, N), F32),
        ),
        out_specs=(pl.BlockSpec(memory_space=pltpu.HBM),) * 3,
        scratch_shapes=[pltpu.VMEM((rows, N), F32)]
        + [square] * 4
        + [pltpu.SemaphoreType.DMA((2 + PARTS,))],
        compiler_params=pltpu.CompilerParams(vmem_limit_bytes=48 << 20),
    )(own, other, snapshots, basis)


def body(snapshots, basis):
    group, chips, cores = (lax.axis_size(a) for a in ("grp", "chip", "core"))
    local = local_products(snapshots, basis, group * chips * cores)
    parts = lax.all_to_all(local, ("chip", "core"), 0, 0)
    mine = sum_and_copy(parts, group)
    parts = lax.all_to_all(mine, "grp", 0, 0)
    mine = sum_and_copy(parts, chips)
    own = lax.all_to_all(mine, "chip", 0, 0)
    other = lax.ppermute(own, "core", [(0, 1), (1, 0)])
    return finish(own, other, snapshots, basis)


def solution(mesh):
    group, many = mesh.devices.shape
    cores = Mesh(mesh.devices.reshape(group, many // 2, 2), ("grp", "chip", "core"))
    rows = P(("grp", "chip", "core"), None)
    return jax.shard_map(
        body,
        mesh=cores,
        in_specs=(rows, rows),
        out_specs=(rows, P(), P()),
        check_vma=False,
    )
```

```python
import functools

import jax
import jax.numpy as jnp
from jax import lax
from jax.experimental import pallas as pl
from jax.experimental.pallas import tpu as pltpu
from jax.sharding import PartitionSpec as P

HIGHEST = lax.Precision.HIGHEST
F32, BF16 = jnp.float32, jnp.bfloat16
N = 128
TILE = 8
TILES = N // TILE


def two_sum(a, b):
    s = a + b
    t = s - a
    return s, (a - (s - t)) + (b - t)


def pair_sum(a, b):
    s, e = two_sum(a[0], b[0])
    return s, e + (a[1] + b[1])


def normal(a):
    s = a[0] + a[1]
    return s, a[1] - (s - a[0])


def dot_t(a, b, precision=None):
    return lax.dot_general(
        a, b, (((0,), (0,)), ((), ())), precision=precision, preferred_element_type=F32
    )


def dot(a, b, precision=None):
    return jnp.dot(a, b, precision=precision, preferred_element_type=F32)


def slices(hi, lo, axis, count, shift):
    step = jnp.max(jnp.abs(hi), axis=axis, keepdims=True) * (2.0**shift)
    first = (hi + step) - step
    rest = hi - first
    step = step * 2.0**-8
    second = (rest + step) - step
    rest = rest - second
    if lo is not None:
        rest = rest + lo
    out = [first.astype(BF16), second.astype(BF16)]
    while len(out) < count:
        part = rest.astype(BF16)
        rest = rest - part.astype(F32)
        out.append(part)
    return out


def exact_dot(left, right):
    wide = jnp.concatenate(left, axis=1)
    tall = jnp.concatenate(right[::-1], axis=0)
    n = len(left)
    terms = [dot(wide[:, : N * k], tall[N * (n - k) :, :]) for k in range(1, n + 1)]
    low = terms[-1]
    for t in terms[-2:1:-1]:
        low = low + t
    s, e = two_sum(terms[0], terms[1])
    return s, e + low


def grid(rows=N):
    return (
        lax.broadcasted_iota(jnp.int32, (rows, N), 0),
        lax.broadcasted_iota(jnp.int32, (rows, N), 1),
    )


def put_diagonal(rest, diagonal):
    row, col = grid(N // 2)
    near = pltpu.roll(diagonal[N // 2 :, :], N - N // 4, 1)
    far = pltpu.roll(diagonal[: N // 2, :], N // 2, 1)
    top = jnp.where(col == row + N // 4, near, rest[: N // 2, :])
    top = jnp.where(col == row + N // 2, far, top)
    return jnp.concatenate([top, rest[N // 2 :, :]], axis=0)


def take_diagonal(rest):
    row, col = grid(N // 2)
    top = rest[: N // 2, :]
    near, far = col == row + N // 4, col == row + N // 2
    first = pltpu.roll(jnp.where(far, top, 0.0), N // 2, 1)
    last = pltpu.roll(jnp.where(near, top, 0.0), N // 4, 1)
    top = jnp.where(near | far, 0.0, top)
    return (
        jnp.concatenate([first, last], axis=0),
        jnp.concatenate([top, rest[N // 2 :, :]], axis=0),
    )


def pack(hi, lo):
    hi, lo = hi.reshape(TILES, TILE, N), lo.reshape(TILES, TILE, N)
    upper = lax.broadcasted_iota(jnp.int32, hi.shape, 1) < TILE // 2
    even = jnp.where(upper, hi, pltpu.roll(lo, TILE // 2, 1))
    odd = jnp.where(upper, pltpu.roll(hi, TILE // 2, 1), lo)
    return jnp.stack([even, odd], axis=1).reshape(2 * TILES, TILE, N)


def unpack(pieces):
    pieces = pieces.reshape(TILES, 2, TILE, N)
    even, odd = pieces[:, 0], pieces[:, 1]
    upper = lax.broadcasted_iota(jnp.int32, even.shape, 1) < TILE // 2
    hi = jnp.where(upper, even, pltpu.roll(odd, TILE // 2, 1))
    lo = jnp.where(upper, pltpu.roll(even, TILE // 2, 1), odd)
    return hi.reshape(N, N), lo.reshape(N, N)


def local_kernel(share, total, z_ref, out_ref):
    a, b, c, d = slices(z_ref[...], None, 0, 4, 17)
    main = dot_t(a, a)
    low_1 = dot_t(a, b)
    low_2 = dot_t(a, c) + 0.5 * dot_t(b, b)
    low_3 = dot_t(a, d) + dot_t(b, c)
    low_4 = dot_t(b, d) + 0.5 * dot_t(c, c)
    half = low_1 + (low_2 + (low_3 + low_4))
    hi, lo = two_sum(main, half + half.T)
    hi, lo = hi * (1.0 / total), lo * (1.0 / total)
    row, col = grid()
    diagonal = jnp.where(row == col, (hi[:N, :N] - share) + lo[:N, :N], 0.0)
    mixed_hi = jnp.where(row < col, hi[:N, :N], hi[N:, N:])
    mixed_lo = put_diagonal(jnp.where(row < col, lo[:N, :N], lo[N:, N:]), diagonal)
    out_ref[: 2 * TILES] = pack(mixed_hi, mixed_lo)
    out_ref[2 * TILES :] = pack(hi[:N, N:], lo[:N, N:])


def local_products(snapshots, basis, devices):
    rows = snapshots.shape[0]
    total = rows * devices
    return pl.pallas_call(
        functools.partial(local_kernel, 1.0 / devices, total),
        out_shape=jax.ShapeDtypeStruct((4 * TILES, TILE, N), F32),
        compiler_params=pltpu.CompilerParams(vmem_limit_bytes=32 << 20),
    )(jnp.concatenate([basis, snapshots], axis=1))


def sum_kernel(in_ref, out_ref):
    parts = [(in_ref[i], None) for i in range(in_ref.shape[0])]
    while len(parts) > 1:
        added = []
        for (a, a_left), (b, b_left) in zip(parts[::2], parts[1::2]):
            s, left = two_sum(a, b)
            if a_left is not None:
                left = left + (a_left + b_left)
            added.append((s, left))
        parts = added
    s, left = parts[0]
    lower = lax.broadcasted_iota(jnp.int32, s.shape, 0) >= TILE // 2
    s = s + jnp.where(lower, pltpu.roll(left, TILE // 2, 0), 0.0)
    for i in range(out_ref.shape[0]):
        out_ref[i] = s


def sum_and_copy(parts, copies):
    return pl.pallas_call(
        sum_kernel,
        out_shape=jax.ShapeDtypeStruct((copies, TILE, N), F32),
        compiler_params=pltpu.CompilerParams(vmem_limit_bytes=32 << 20),
    )(parts)


def spread_row(tile, k):
    return jnp.broadcast_to(tile[k : k + 1, :], (TILE, N))


def spread_lane(tile, j):
    return jnp.broadcast_to(tile[:, j : j + 1], (TILE, N))


def factor_inverse(gram):
    sub = lax.broadcasted_iota(jnp.int32, (TILE, N), 0)
    lane = lax.broadcasted_iota(jnp.int32, (TILE, N), 1)
    work = [gram[q * TILE : (q + 1) * TILE, :] for q in range(TILES)]
    upper, inverse = [], []
    for p in range(TILES):
        at, after = p * TILE, range(p + 1, TILES)
        d = {}
        for j in range(TILE):
            column = spread_lane(work[p], at + j)
            for i in range(j + 1):
                d[i, j] = spread_row(column, i)
        below = {(q, j): spread_lane(work[q], at + j) for q in after for j in range(TILE)}
        right = lane >= at + TILE
        block = (lane >= at) & (lane < at + TILE)
        for q in after:
            work[q] = jnp.where(block, 0.0, work[q])
        left = jnp.where(lane < at, work[p], jnp.where(lane == at + sub, 1.0, 0.0))
        rows = [(spread_row(work[p], k), spread_row(left, k)) for k in range(TILE)]
        new = [jnp.zeros((TILE, N), F32)] * 2
        for k in range(TILE):
            scale = lax.rsqrt(d[k, k])
            for j in range(k + 1, TILE):
                d[k, j] = d[k, j] * scale
            for i in range(k + 1, TILE):
                for j in range(i, TILE):
                    d[i, j] = d[i, j] - d[k, i] * d[k, j]
            row = (rows[k][0] * scale, rows[k][1] * scale)
            for i in range(k + 1, TILE):
                rows[i] = tuple(a - d[k, i] * b for a, b in zip(rows[i], row))
            finished = jnp.where(right, *row)
            for q in after:
                m = below[q, k] * scale
                for j in range(k + 1, TILE):
                    below[q, j] = below[q, j] - m * d[k, j]
                work[q] = work[q] - m * finished
            new = [jnp.where(sub == k, a, b) for a, b in zip(row, new)]
        upper.append(jnp.where(lane >= at + sub, new[0], 0.0))
        inverse.append(jnp.where(right, 0.0, new[1]))
    return jnp.concatenate(upper, axis=0), jnp.concatenate(inverse, axis=0)


def three_dot_t(left, right):
    l1, r1 = left.astype(BF16), right.astype(BF16)
    l2 = (left - l1.astype(F32)).astype(BF16)
    r2 = (right - r1.astype(F32)).astype(BF16)
    return dot_t(jnp.concatenate([l1, l1, l2], 0), jnp.concatenate([r1, r2, r1], 0))


def three_dot(left, right):
    l1, r1 = left.astype(BF16), right.astype(BF16)
    l2 = (left - l1.astype(F32)).astype(BF16)
    r2 = (right - r1.astype(F32)).astype(BF16)
    return dot(jnp.concatenate([l1, l1, l2], 1), jnp.concatenate([r1, r2, r1], 0))


NEAR = 2.0**-4
TURNS = 4


def near_factor(off, inv_one):
    row, col = grid()
    weight = jnp.where(row < col, 1.0, jnp.where(row == col, 0.5, 0.0))
    n = off * weight
    for _ in range(TURNS):
        n = (off - three_dot_t(n, n)) * weight
    first = inv_one - dot(inv_one, n, HIGHEST)
    n2 = three_dot(n, n)
    n2 = n2 + three_dot(n2, n2)
    return jnp.where(row == col, 1.0, 0.0) + n, first + three_dot(first, n2)


PARTS = 4


def final_kernel(sums_ref, snap_ref, basis_ref, modes_hbm, factor_hbm, coef_hbm,
                 modes_ref, factor_ref, coef_ref, u_ref, t_ref, sem):
    row, col = grid()
    mixed_hi, mixed_lo = unpack(sums_ref[: 2 * TILES])
    cross = unpack(sums_ref[2 * TILES :])
    diagonal, mixed_lo = take_diagonal(mixed_lo)
    turned_hi, turned_lo = mixed_hi.T, mixed_lo.T
    one = jnp.where(row == col, 1.0, 0.0)
    one_hi, one_lo = two_sum(one, diagonal)
    basis_gram = (
        jnp.where(row == col, one_hi, jnp.where(row < col, mixed_hi, turned_hi)),
        jnp.where(row == col, one_lo, jnp.where(row < col, mixed_lo, turned_lo)),
    )
    snap_gram = (
        jnp.where(row < col, turned_hi, mixed_hi),
        jnp.where(row < col, turned_lo, mixed_lo),
    )
    coef_two = cross[0] - dot(basis_gram[0], cross[0], HIGHEST)
    coef = cross[0] + coef_two
    coef_ref[...] = coef
    coef_copy = pltpu.make_async_copy(coef_ref, coef_hbm, sem.at[0])
    coef_copy.start()
    second = snap_ref[...] - dot(basis_ref[...], coef, HIGHEST)

    g_c = exact_dot(slices(*basis_gram, 1, 5, 16), slices(coef, None, 0, 5, 16))
    held = pair_sum((2.0 * cross[0], 2.0 * cross[1]), (-g_c[0], -g_c[1]))
    held = normal(held)
    c_h = exact_dot(slices(coef.T, None, 1, 5, 16), slices(*held, 0, 5, 16))
    c_h = pair_sum((0.5 * c_h[0], 0.5 * c_h[1]), (0.5 * c_h[0].T, 0.5 * c_h[1].T))
    gram_one = normal(pair_sum(snap_gram, (-c_h[0], -c_h[1])))

    upper_one, inv_one_t = factor_inverse(gram_one[0])
    inv_one = inv_one_t.T
    g_i = exact_dot(slices(*gram_one, 1, 5, 16), slices(inv_one, None, 0, 5, 16))
    g_i = normal(g_i)
    i_g_i = exact_dot(slices(inv_one_t, None, 1, 5, 16), slices(*g_i, 0, 5, 16))
    off = (i_g_i[0] - one) + i_g_i[1]
    is_near = jnp.sum(off * off) <= NEAR * NEAR

    u_ref[...], t_ref[...] = near_factor(off, inv_one)

    @pl.when(jnp.logical_not(is_near))
    def _():
        upper, inv_t = factor_inverse(one + off)
        u_ref[...] = upper
        t_ref[...] = dot(inv_one, inv_t.T, HIGHEST)

    both = t_ref[...]
    copies = [coef_copy]
    step = modes_ref.shape[0] // PARTS
    for i in range(PARTS):
        part = slice(i * step, (i + 1) * step)
        modes_ref[part, :] = dot(second[part, :], both, HIGHEST)
        copies.append(
            pltpu.make_async_copy(modes_ref.at[part, :], modes_hbm.at[part, :], sem.at[2 + i])
        )
        copies[-1].start()
        if i == 0:
            factor_ref[...] = dot(u_ref[...], upper_one, HIGHEST)
            copies.append(pltpu.make_async_copy(factor_ref, factor_hbm, sem.at[1]))
            copies[-1].start()
    for copy in copies:
        copy.wait()


def finish(sums, snapshots, basis):
    rows = snapshots.shape[0]
    square = pltpu.VMEM((N, N), F32)
    return pl.pallas_call(
        final_kernel,
        out_shape=(
            jax.ShapeDtypeStruct((rows, N), F32),
            jax.ShapeDtypeStruct((N, N), F32),
            jax.ShapeDtypeStruct((N, N), F32),
        ),
        out_specs=(pl.BlockSpec(memory_space=pltpu.HBM),) * 3,
        scratch_shapes=[pltpu.VMEM((rows, N), F32)]
        + [square] * 4
        + [pltpu.SemaphoreType.DMA((2 + PARTS,))],
        compiler_params=pltpu.CompilerParams(vmem_limit_bytes=48 << 20),
    )(sums, snapshots, basis)


def body(snapshots, basis):
    group, many = lax.axis_size("grp"), lax.axis_size("dev")
    local = local_products(snapshots, basis, group * many)
    parts = lax.all_to_all(local, "dev", 0, 0)
    mine = sum_and_copy(parts, group)
    parts = lax.all_to_all(mine, "grp", 0, 0)
    mine = sum_and_copy(parts, many)
    sums = lax.all_to_all(mine, "dev", 0, 0)
    return finish(sums, snapshots, basis)


def solution(mesh):
    return jax.shard_map(
        body,
        mesh=mesh,
        in_specs=(P(("grp", "dev"), None), P(("grp", "dev"), None)),
        out_specs=(P(("grp", "dev"), None), P(), P()),
        check_vma=False,
    )
```

```python
import functools

import jax
import jax.numpy as jnp
from jax import lax
from jax.experimental import pallas as pl
from jax.experimental.pallas import tpu as pltpu
from jax.sharding import PartitionSpec as P

HIGHEST = lax.Precision.HIGHEST
F32, BF16 = jnp.float32, jnp.bfloat16
N = 128
TILE = 8
TILES = N // TILE


def two_sum(a, b):
    s = a + b
    t = s - a
    return s, (a - (s - t)) + (b - t)


def pair_sum(a, b):
    s, e = two_sum(a[0], b[0])
    return s, e + (a[1] + b[1])


def normal(a):
    s = a[0] + a[1]
    return s, a[1] - (s - a[0])


def dot_t(a, b, precision=None):
    return lax.dot_general(
        a, b, (((0,), (0,)), ((), ())), precision=precision, preferred_element_type=F32
    )


def dot(a, b, precision=None):
    return jnp.dot(a, b, precision=precision, preferred_element_type=F32)


def slices(hi, lo, axis, count, shift):
    step = jnp.max(jnp.abs(hi), axis=axis, keepdims=True) * (2.0**shift)
    first = (hi + step) - step
    rest = hi - first
    step = step * 2.0**-8
    second = (rest + step) - step
    rest = rest - second
    if lo is not None:
        rest = rest + lo
    out = [first.astype(BF16), second.astype(BF16)]
    while len(out) < count:
        part = rest.astype(BF16)
        rest = rest - part.astype(F32)
        out.append(part)
    return out


def exact_dot(left, right):
    wide = jnp.concatenate(left, axis=1)
    tall = jnp.concatenate(right[::-1], axis=0)
    n = len(left)
    terms = [dot(wide[:, : N * k], tall[N * (n - k) :, :]) for k in range(1, n + 1)]
    low = terms[-1]
    for t in terms[-2:1:-1]:
        low = low + t
    s, e = two_sum(terms[0], terms[1])
    return s, e + low


def grid(rows=N):
    return (
        lax.broadcasted_iota(jnp.int32, (rows, N), 0),
        lax.broadcasted_iota(jnp.int32, (rows, N), 1),
    )


def put_diagonal(rest, diagonal):
    row, col = grid(N // 2)
    near = pltpu.roll(diagonal[N // 2 :, :], N - N // 4, 1)
    far = pltpu.roll(diagonal[: N // 2, :], N // 2, 1)
    top = jnp.where(col == row + N // 4, near, rest[: N // 2, :])
    top = jnp.where(col == row + N // 2, far, top)
    return jnp.concatenate([top, rest[N // 2 :, :]], axis=0)


def take_diagonal(rest):
    row, col = grid(N // 2)
    top = rest[: N // 2, :]
    near, far = col == row + N // 4, col == row + N // 2
    first = pltpu.roll(jnp.where(far, top, 0.0), N // 2, 1)
    last = pltpu.roll(jnp.where(near, top, 0.0), N // 4, 1)
    top = jnp.where(near | far, 0.0, top)
    return (
        jnp.concatenate([first, last], axis=0),
        jnp.concatenate([top, rest[N // 2 :, :]], axis=0),
    )


def pack(hi, lo):
    hi, lo = hi.reshape(TILES, TILE, N), lo.reshape(TILES, TILE, N)
    upper = lax.broadcasted_iota(jnp.int32, hi.shape, 1) < TILE // 2
    even = jnp.where(upper, hi, pltpu.roll(lo, TILE // 2, 1))
    odd = jnp.where(upper, pltpu.roll(hi, TILE // 2, 1), lo)
    return jnp.stack([even, odd], axis=1).reshape(2 * TILES, TILE, N)


def unpack(pieces):
    pieces = pieces.reshape(TILES, 2, TILE, N)
    even, odd = pieces[:, 0], pieces[:, 1]
    upper = lax.broadcasted_iota(jnp.int32, even.shape, 1) < TILE // 2
    hi = jnp.where(upper, even, pltpu.roll(odd, TILE // 2, 1))
    lo = jnp.where(upper, pltpu.roll(even, TILE // 2, 1), odd)
    return hi.reshape(N, N), lo.reshape(N, N)


def local_kernel(share, total, z_ref, out_ref):
    a, b, c, d = slices(z_ref[...], None, 0, 4, 17)
    main = dot_t(a, a)
    low_1 = dot_t(a, b)
    low_2 = dot_t(a, c) + 0.5 * dot_t(b, b)
    low_3 = dot_t(a, d) + dot_t(b, c)
    low_4 = dot_t(b, d) + 0.5 * dot_t(c, c)
    half = low_1 + (low_2 + (low_3 + low_4))
    hi, lo = two_sum(main, half + half.T)
    hi, lo = hi * (1.0 / total), lo * (1.0 / total)
    row, col = grid()
    diagonal = jnp.where(row == col, (hi[:N, :N] - share) + lo[:N, :N], 0.0)
    mixed_hi = jnp.where(row < col, hi[:N, :N], hi[N:, N:])
    mixed_lo = put_diagonal(jnp.where(row < col, lo[:N, :N], lo[N:, N:]), diagonal)
    out_ref[: 2 * TILES] = pack(mixed_hi, mixed_lo)
    out_ref[2 * TILES :] = pack(hi[:N, N:], lo[:N, N:])


def local_products(snapshots, basis, devices):
    rows = snapshots.shape[0]
    total = rows * devices
    return pl.pallas_call(
        functools.partial(local_kernel, 1.0 / devices, total),
        out_shape=jax.ShapeDtypeStruct((4 * TILES, TILE, N), F32),
        compiler_params=pltpu.CompilerParams(vmem_limit_bytes=32 << 20),
    )(jnp.concatenate([basis, snapshots], axis=1))


def sum_kernel(in_ref, out_ref):
    parts = [(in_ref[i], None) for i in range(in_ref.shape[0])]
    while len(parts) > 1:
        added = []
        for (a, a_left), (b, b_left) in zip(parts[::2], parts[1::2]):
            s, left = two_sum(a, b)
            if a_left is not None:
                left = left + (a_left + b_left)
            added.append((s, left))
        parts = added
    s, left = parts[0]
    lower = lax.broadcasted_iota(jnp.int32, s.shape, 0) >= TILE // 2
    s = s + jnp.where(lower, pltpu.roll(left, TILE // 2, 0), 0.0)
    for i in range(out_ref.shape[0]):
        out_ref[i] = s


def sum_and_copy(parts, copies):
    return pl.pallas_call(
        sum_kernel,
        out_shape=jax.ShapeDtypeStruct((copies, TILE, N), F32),
        compiler_params=pltpu.CompilerParams(vmem_limit_bytes=32 << 20),
    )(parts)


def spread_row(tile, k):
    return jnp.broadcast_to(tile[k : k + 1, :], (TILE, N))


def spread_lane(tile, j):
    return jnp.broadcast_to(tile[:, j : j + 1], (TILE, N))


AHEAD = 1


def spread_ref(ref, p, k):
    return jnp.broadcast_to(ref[p, k : k + 1, :], (TILE, N))


def factor_inverse(gram, scr):
    sub = lax.broadcasted_iota(jnp.int32, (TILE, N), 0)
    lane = lax.broadcasted_iota(jnp.int32, (TILE, N), 1)
    work = [gram[q * TILE : (q + 1) * TILE, :] for q in range(TILES)]
    upper, inverse = [], []
    for p in range(TILES):
        at, after = p * TILE, range(p + 1, TILES)
        near, far = after[:AHEAD], after[AHEAD:]
        d = {}
        for j in range(TILE):
            scr[p, TILE * j : TILE * j + TILE, :] = spread_lane(work[p], at + j)
            for i in range(j + 1):
                d[i, j] = spread_ref(scr, p, TILE * j + i)
        below = {(q, j): spread_lane(work[q], at + j) for q in near for j in range(TILE)}
        right = lane >= at + TILE
        block = (lane >= at) & (lane < at + TILE)
        for q in after:
            work[q] = jnp.where(block, 0.0, work[q])
        left = jnp.where(lane < at, work[p], jnp.where(lane == at + sub, 1.0, 0.0))
        rows = [(spread_row(work[p], k), spread_row(left, k)) for k in range(TILE)]
        new = [jnp.zeros((TILE, N), F32)] * 2
        for k in range(TILE):
            scale = lax.rsqrt(d[k, k])
            for j in range(k + 1, TILE):
                d[k, j] = d[k, j] * scale
            for i in range(k + 1, TILE):
                for j in range(i, TILE):
                    d[i, j] = d[i, j] - d[k, i] * d[k, j]
            row = (rows[k][0] * scale, rows[k][1] * scale)
            for i in range(k + 1, TILE):
                rows[i] = tuple(a - d[k, i] * b for a, b in zip(rows[i], row))
            finished = jnp.where(right, *row)
            for q in near:
                m = below[q, k] * scale
                for j in range(k + 1, TILE):
                    below[q, j] = below[q, j] - m * d[k, j]
                work[q] = work[q] - m * finished
            for q in far:
                m = jnp.take_along_axis(row[0], sub + q * TILE, axis=1)
                work[q] = work[q] - m * finished
            new = [jnp.where(sub == k, a, b) for a, b in zip(row, new)]
        upper.append(jnp.where(lane >= at + sub, new[0], 0.0))
        inverse.append(jnp.where(right, 0.0, new[1]))
    return jnp.concatenate(upper, axis=0), jnp.concatenate(inverse, axis=0)


def three_square(a):
    hi = a.astype(BF16)
    lo = (a - hi.astype(F32)).astype(BF16)
    return lax.dot_general(
        jnp.concatenate([hi, hi, lo], 1),
        jnp.concatenate([hi, lo, hi], 1),
        (((1,), (1,)), ((), ())),
        preferred_element_type=F32,
    )


def three_dot(left, right):
    l1, r1 = left.astype(BF16), right.astype(BF16)
    l2 = (left - l1.astype(F32)).astype(BF16)
    r2 = (right - r1.astype(F32)).astype(BF16)
    return dot(jnp.concatenate([l1, l1, l2], 1), jnp.concatenate([r1, r2, r1], 0))


NEAR = 2.0**-4
TURNS = 4


def near_factor(off, inv_one):
    row, col = grid()
    weight = jnp.where(row > col, 1.0, jnp.where(row == col, 0.5, 0.0))
    low = off * weight
    for _ in range(TURNS):
        low = (off - three_square(low)) * weight
    n = low.T
    first = inv_one - dot(inv_one, n, HIGHEST)
    n2 = three_dot(n, n)
    n2 = n2 + three_dot(n2, n2)
    return jnp.where(row == col, 1.0, 0.0) + n, first + three_dot(first, n2)


PARTS = 4


def final_kernel(sums_ref, snap_ref, basis_ref, modes_hbm, factor_hbm, coef_hbm,
                 modes_ref, factor_ref, coef_ref, u_ref, t_ref, sem, scr):
    row, col = grid()
    mixed_hi, mixed_lo = unpack(sums_ref[: 2 * TILES])
    cross = unpack(sums_ref[2 * TILES :])
    diagonal, mixed_lo = take_diagonal(mixed_lo)
    turned_hi, turned_lo = mixed_hi.T, mixed_lo.T
    one = jnp.where(row == col, 1.0, 0.0)
    one_hi, one_lo = two_sum(one, diagonal)
    basis_gram = (
        jnp.where(row == col, one_hi, jnp.where(row < col, mixed_hi, turned_hi)),
        jnp.where(row == col, one_lo, jnp.where(row < col, mixed_lo, turned_lo)),
    )
    snap_gram = (
        jnp.where(row < col, turned_hi, mixed_hi),
        jnp.where(row < col, turned_lo, mixed_lo),
    )
    coef_two = cross[0] - dot(basis_gram[0], cross[0], HIGHEST)
    coef = cross[0] + coef_two
    coef_ref[...] = coef
    coef_copy = pltpu.make_async_copy(coef_ref, coef_hbm, sem.at[0])
    coef_copy.start()
    second = snap_ref[...] - dot(basis_ref[...], coef, HIGHEST)

    g_c = exact_dot(slices(*basis_gram, 1, 5, 16), slices(coef, None, 0, 5, 16))
    held = pair_sum((2.0 * cross[0], 2.0 * cross[1]), (-g_c[0], -g_c[1]))
    held = normal(held)
    c_h = exact_dot(slices(coef.T, None, 1, 5, 16), slices(*held, 0, 5, 16))
    c_h = pair_sum((0.5 * c_h[0], 0.5 * c_h[1]), (0.5 * c_h[0].T, 0.5 * c_h[1].T))
    gram_one = normal(pair_sum(snap_gram, (-c_h[0], -c_h[1])))

    upper_one, inv_one_t = factor_inverse(gram_one[0], scr)
    inv_one = inv_one_t.T
    g_i = exact_dot(slices(*gram_one, 1, 5, 16), slices(inv_one, None, 0, 5, 16))
    g_i = normal(g_i)
    i_g_i = exact_dot(slices(inv_one_t, None, 1, 5, 16), slices(*g_i, 0, 5, 16))
    off = (i_g_i[0] - one) + i_g_i[1]
    is_near = jnp.sum(off * off) <= NEAR * NEAR

    u_ref[...], t_ref[...] = near_factor(off, inv_one)

    @pl.when(jnp.logical_not(is_near))
    def _():
        upper, inv_t = factor_inverse(one + off, scr)
        u_ref[...] = upper
        t_ref[...] = dot(inv_one, inv_t.T, HIGHEST)

    both = t_ref[...]
    copies = [coef_copy]
    step = modes_ref.shape[0] // PARTS
    for i in range(PARTS):
        part = slice(i * step, (i + 1) * step)
        modes_ref[part, :] = dot(second[part, :], both, HIGHEST)
        copies.append(
            pltpu.make_async_copy(modes_ref.at[part, :], modes_hbm.at[part, :], sem.at[2 + i])
        )
        copies[-1].start()
        if i == 0:
            factor_ref[...] = dot(u_ref[...], upper_one, HIGHEST)
            copies.append(pltpu.make_async_copy(factor_ref, factor_hbm, sem.at[1]))
            copies[-1].start()
    for copy in copies:
        copy.wait()


def finish(sums, snapshots, basis):
    rows = snapshots.shape[0]
    square = pltpu.VMEM((N, N), F32)
    return pl.pallas_call(
        final_kernel,
        out_shape=(
            jax.ShapeDtypeStruct((rows, N), F32),
            jax.ShapeDtypeStruct((N, N), F32),
            jax.ShapeDtypeStruct((N, N), F32),
        ),
        out_specs=(pl.BlockSpec(memory_space=pltpu.HBM),) * 3,
        scratch_shapes=[pltpu.VMEM((rows, N), F32)]
        + [square] * 4
        + [pltpu.SemaphoreType.DMA((2 + PARTS,)), pltpu.VMEM((TILES, TILE * TILE, N), F32)],
        compiler_params=pltpu.CompilerParams(vmem_limit_bytes=48 << 20),
    )(sums, snapshots, basis)


def body(snapshots, basis):
    group, many = lax.axis_size("grp"), lax.axis_size("dev")
    local = local_products(snapshots, basis, group * many)
    parts = lax.all_to_all(local, "dev", 0, 0)
    mine = sum_and_copy(parts, group)
    parts = lax.all_to_all(mine, "grp", 0, 0)
    mine = sum_and_copy(parts, many)
    sums = lax.all_to_all(mine, "dev", 0, 0)
    return finish(sums, snapshots, basis)


def solution(mesh):
    return jax.shard_map(
        body,
        mesh=mesh,
        in_specs=(P(("grp", "dev"), None), P(("grp", "dev"), None)),
        out_specs=(P(("grp", "dev"), None), P(), P()),
        check_vma=False,
    )
```

```python
import functools

import jax
import jax.numpy as jnp
from jax import lax
from jax.experimental import pallas as pl
from jax.experimental.pallas import tpu as pltpu
from jax.sharding import PartitionSpec as P

HIGHEST = lax.Precision.HIGHEST
F32, BF16 = jnp.float32, jnp.bfloat16
N = 128
TILE = 8
TILES = N // TILE


def two_sum(a, b):
    s = a + b
    t = s - a
    return s, (a - (s - t)) + (b - t)


def pair_sum(a, b):
    s, e = two_sum(a[0], b[0])
    return s, e + (a[1] + b[1])


def normal(a):
    s = a[0] + a[1]
    return s, a[1] - (s - a[0])


def dot_t(a, b, precision=None):
    return lax.dot_general(
        a, b, (((0,), (0,)), ((), ())), precision=precision, preferred_element_type=F32
    )


def dot(a, b, precision=None):
    return jnp.dot(a, b, precision=precision, preferred_element_type=F32)


def slices(hi, lo, axis, count, shift):
    step = jnp.max(jnp.abs(hi), axis=axis, keepdims=True) * (2.0**shift)
    first = (hi + step) - step
    rest = hi - first
    step = step * 2.0**-8
    second = (rest + step) - step
    rest = rest - second
    if lo is not None:
        rest = rest + lo
    out = [first.astype(BF16), second.astype(BF16)]
    while len(out) < count:
        part = rest.astype(BF16)
        rest = rest - part.astype(F32)
        out.append(part)
    return out


def exact_dot(left, right):
    wide = jnp.concatenate(left, axis=1)
    tall = jnp.concatenate(right[::-1], axis=0)
    n = len(left)
    terms = [dot(wide[:, : N * k], tall[N * (n - k) :, :]) for k in range(1, n + 1)]
    low = terms[-1]
    for t in terms[-2:1:-1]:
        low = low + t
    s, e = two_sum(terms[0], terms[1])
    return s, e + low


def grid(rows=N):
    return (
        lax.broadcasted_iota(jnp.int32, (rows, N), 0),
        lax.broadcasted_iota(jnp.int32, (rows, N), 1),
    )


def put_diagonal(rest, diagonal):
    row, col = grid(N // 2)
    near = pltpu.roll(diagonal[N // 2 :, :], N - N // 4, 1)
    far = pltpu.roll(diagonal[: N // 2, :], N // 2, 1)
    top = jnp.where(col == row + N // 4, near, rest[: N // 2, :])
    top = jnp.where(col == row + N // 2, far, top)
    return jnp.concatenate([top, rest[N // 2 :, :]], axis=0)


def take_diagonal(rest):
    row, col = grid(N // 2)
    top = rest[: N // 2, :]
    near, far = col == row + N // 4, col == row + N // 2
    first = pltpu.roll(jnp.where(far, top, 0.0), N // 2, 1)
    last = pltpu.roll(jnp.where(near, top, 0.0), N // 4, 1)
    top = jnp.where(near | far, 0.0, top)
    return (
        jnp.concatenate([first, last], axis=0),
        jnp.concatenate([top, rest[N // 2 :, :]], axis=0),
    )


def pack(hi, lo):
    hi, lo = hi.reshape(TILES, TILE, N), lo.reshape(TILES, TILE, N)
    upper = lax.broadcasted_iota(jnp.int32, hi.shape, 1) < TILE // 2
    even = jnp.where(upper, hi, pltpu.roll(lo, TILE // 2, 1))
    odd = jnp.where(upper, pltpu.roll(hi, TILE // 2, 1), lo)
    return jnp.stack([even, odd], axis=1).reshape(2 * TILES, TILE, N)


def unpack(pieces):
    pieces = pieces.reshape(TILES, 2, TILE, N)
    even, odd = pieces[:, 0], pieces[:, 1]
    upper = lax.broadcasted_iota(jnp.int32, even.shape, 1) < TILE // 2
    hi = jnp.where(upper, even, pltpu.roll(odd, TILE // 2, 1))
    lo = jnp.where(upper, pltpu.roll(even, TILE // 2, 1), odd)
    return hi.reshape(N, N), lo.reshape(N, N)


def local_kernel(share, total, z_ref, out_ref):
    a, b, c, d = slices(z_ref[...], None, 0, 4, 17)
    main = dot_t(a, a)
    low_1 = dot_t(a, b)
    low_2 = dot_t(a, c) + 0.5 * dot_t(b, b)
    low_3 = dot_t(a, d) + dot_t(b, c)
    low_4 = dot_t(b, d) + 0.5 * dot_t(c, c)
    half = low_1 + (low_2 + (low_3 + low_4))
    hi, lo = two_sum(main, half + half.T)
    hi, lo = hi * (1.0 / total), lo * (1.0 / total)
    row, col = grid()
    diagonal = jnp.where(row == col, (hi[:N, :N] - share) + lo[:N, :N], 0.0)
    mixed_hi = jnp.where(row < col, hi[:N, :N], hi[N:, N:])
    mixed_lo = put_diagonal(jnp.where(row < col, lo[:N, :N], lo[N:, N:]), diagonal)
    out_ref[: 2 * TILES] = pack(mixed_hi, mixed_lo)
    out_ref[2 * TILES :] = pack(hi[:N, N:], lo[:N, N:])


def local_products(snapshots, basis, devices):
    rows = snapshots.shape[0]
    total = rows * devices
    return pl.pallas_call(
        functools.partial(local_kernel, 1.0 / devices, total),
        out_shape=jax.ShapeDtypeStruct((4 * TILES, TILE, N), F32),
        compiler_params=pltpu.CompilerParams(vmem_limit_bytes=32 << 20),
    )(jnp.concatenate([basis, snapshots], axis=1))


def sum_kernel(in_ref, out_ref):
    parts = [(in_ref[i], None) for i in range(in_ref.shape[0])]
    while len(parts) > 1:
        added = []
        for (a, a_left), (b, b_left) in zip(parts[::2], parts[1::2]):
            s, left = two_sum(a, b)
            if a_left is not None:
                left = left + (a_left + b_left)
            added.append((s, left))
        parts = added
    s, left = parts[0]
    lower = lax.broadcasted_iota(jnp.int32, s.shape, 0) >= TILE // 2
    s = s + jnp.where(lower, pltpu.roll(left, TILE // 2, 0), 0.0)
    for i in range(out_ref.shape[0]):
        out_ref[i] = s


def sum_and_copy(parts, copies):
    return pl.pallas_call(
        sum_kernel,
        out_shape=jax.ShapeDtypeStruct((copies, TILE, N), F32),
        compiler_params=pltpu.CompilerParams(vmem_limit_bytes=32 << 20),
    )(parts)


def spread_row(tile, k):
    return jnp.broadcast_to(tile[k : k + 1, :], (TILE, N))


def spread_lane(tile, j):
    return jnp.broadcast_to(tile[:, j : j + 1], (TILE, N))


AHEAD = 1


def spread_ref(ref, p, k):
    return jnp.broadcast_to(ref[p, k : k + 1, :], (TILE, N))


def factor_inverse(gram, scr):
    sub = lax.broadcasted_iota(jnp.int32, (TILE, N), 0)
    lane = lax.broadcasted_iota(jnp.int32, (TILE, N), 1)
    work = [gram[q * TILE : (q + 1) * TILE, :] for q in range(TILES)]
    upper, inverse = [], []
    for p in range(TILES):
        at, after = p * TILE, range(p + 1, TILES)
        near, far = after[:AHEAD], after[AHEAD:]
        d = {}
        for j in range(TILE):
            scr[p, TILE * j : TILE * j + TILE, :] = spread_lane(work[p], at + j)
            for i in range(j + 1):
                d[i, j] = spread_ref(scr, p, TILE * j + i)
        below = {(q, j): spread_lane(work[q], at + j) for q in near for j in range(TILE)}
        right = lane >= at + TILE
        block = (lane >= at) & (lane < at + TILE)
        for q in after:
            work[q] = jnp.where(block, 0.0, work[q])
        left = jnp.where(lane < at, work[p], jnp.where(lane == at + sub, 1.0, 0.0))
        rows = [(spread_row(work[p], k), spread_row(left, k)) for k in range(TILE)]
        new = [jnp.zeros((TILE, N), F32)] * 2
        for k in range(TILE):
            scale = lax.rsqrt(d[k, k])
            for j in range(k + 1, TILE):
                d[k, j] = d[k, j] * scale
            for i in range(k + 1, TILE):
                for j in range(i, TILE):
                    d[i, j] = d[i, j] - d[k, i] * d[k, j]
            row = (rows[k][0] * scale, rows[k][1] * scale)
            for i in range(k + 1, TILE):
                rows[i] = tuple(a - d[k, i] * b for a, b in zip(rows[i], row))
            finished = jnp.where(right, *row)
            for q in near:
                m = below[q, k] * scale
                for j in range(k + 1, TILE):
                    below[q, j] = below[q, j] - m * d[k, j]
                work[q] = work[q] - m * finished
            for q in far:
                m = jnp.take_along_axis(row[0], sub + q * TILE, axis=1)
                work[q] = work[q] - m * finished
            new = [jnp.where(sub == k, a, b) for a, b in zip(row, new)]
        upper.append(jnp.where(lane >= at + sub, new[0], 0.0))
        inverse.append(jnp.where(right, 0.0, new[1]))
    return jnp.concatenate(upper, axis=0), jnp.concatenate(inverse, axis=0)


def power_near(value):
    p, q = jnp.ones_like(value), jnp.ones_like(value)
    for k in (4, 2, 1):
        large = (value * p) * p > 2.0 ** (2 * k - 1)
        p, q = jnp.where(large, p * 2.0**-k, p), jnp.where(large, q * 2.0**k, q)
    for k in (32, 16, 8, 4, 2, 1):
        small = (value * p) * p < 2.0 ** (1 - 2 * k)
        p, q = jnp.where(small, p * 2.0**k, p), jnp.where(small, q * 2.0**-k, q)
    return p, q


def three_square(a):
    hi = a.astype(BF16)
    lo = (a - hi.astype(F32)).astype(BF16)
    return lax.dot_general(
        jnp.concatenate([hi, hi, lo], 1),
        jnp.concatenate([hi, lo, hi], 1),
        (((1,), (1,)), ((), ())),
        preferred_element_type=F32,
    )


def three_dot(left, right):
    l1, r1 = left.astype(BF16), right.astype(BF16)
    l2 = (left - l1.astype(F32)).astype(BF16)
    r2 = (right - r1.astype(F32)).astype(BF16)
    return dot(jnp.concatenate([l1, l1, l2], 1), jnp.concatenate([r1, r2, r1], 0))


NEAR = 2.0**-4
TURNS = 4


def near_factor(off, inv_one):
    row, col = grid()
    weight = jnp.where(row > col, 1.0, jnp.where(row == col, 0.5, 0.0))
    low = off * weight
    for _ in range(TURNS):
        low = (off - three_square(low)) * weight
    n = low.T
    first = inv_one - dot(inv_one, n, HIGHEST)
    n2 = three_dot(n, n)
    n2 = n2 + three_dot(n2, n2)
    return jnp.where(row == col, 1.0, 0.0) + n, first + three_dot(first, n2)


PARTS = 4


def final_kernel(sums_ref, snap_ref, basis_ref, modes_hbm, factor_hbm, coef_hbm,
                 modes_ref, factor_ref, coef_ref, u_ref, t_ref, sem, scr):
    row, col = grid()
    mixed_hi, mixed_lo = unpack(sums_ref[: 2 * TILES])
    cross = unpack(sums_ref[2 * TILES :])
    diagonal, mixed_lo = take_diagonal(mixed_lo)
    turned_hi, turned_lo = mixed_hi.T, mixed_lo.T
    one = jnp.where(row == col, 1.0, 0.0)
    one_hi, one_lo = two_sum(one, diagonal)
    basis_gram = (
        jnp.where(row == col, one_hi, jnp.where(row < col, mixed_hi, turned_hi)),
        jnp.where(row == col, one_lo, jnp.where(row < col, mixed_lo, turned_lo)),
    )
    snap_gram = (
        jnp.where(row < col, turned_hi, mixed_hi),
        jnp.where(row < col, turned_lo, mixed_lo),
    )
    coef_two = cross[0] - dot(basis_gram[0], cross[0], HIGHEST)
    coef = cross[0] + coef_two
    coef_ref[...] = coef
    coef_copy = pltpu.make_async_copy(coef_ref, coef_hbm, sem.at[0])
    coef_copy.start()
    second = snap_ref[...] - dot(basis_ref[...], coef, HIGHEST)

    g_c = exact_dot(slices(*basis_gram, 1, 5, 16), slices(coef, None, 0, 5, 16))
    held = pair_sum((2.0 * cross[0], 2.0 * cross[1]), (-g_c[0], -g_c[1]))
    held = normal(held)
    c_h = exact_dot(slices(coef.T, None, 1, 5, 16), slices(*held, 0, 5, 16))
    c_h = pair_sum((0.5 * c_h[0], 0.5 * c_h[1]), (0.5 * c_h[0].T, 0.5 * c_h[1].T))
    gram_one = normal(pair_sum(snap_gram, (-c_h[0], -c_h[1])))

    upper_one, inv_one_t = factor_inverse(gram_one[0], scr)
    inv_one = inv_one_t.T
    diagonal = jnp.where(row == col, gram_one[0], 0.0)
    across, back_across = power_near(jnp.sum(diagonal, axis=0, keepdims=True))
    down, back_down = power_near(jnp.sum(diagonal, axis=1, keepdims=True))
    scaled = tuple((part * across) * down for part in gram_one)
    g_i = exact_dot(slices(*scaled, 1, 5, 16), slices(inv_one * back_down, None, 0, 5, 16))
    g_i = normal(g_i)
    i_g_i = exact_dot(slices(inv_one_t * back_across, None, 1, 5, 16), slices(*g_i, 0, 5, 16))
    off = (i_g_i[0] - one) + i_g_i[1]
    is_near = jnp.sum(off * off) <= NEAR * NEAR

    u_ref[...], t_ref[...] = near_factor(off, inv_one)

    @pl.when(jnp.logical_not(is_near))
    def _():
        upper, inv_t = factor_inverse(one + off, scr)
        u_ref[...] = upper
        t_ref[...] = dot(inv_one, inv_t.T, HIGHEST)

    both = t_ref[...]
    copies = [coef_copy]
    step = modes_ref.shape[0] // PARTS
    for i in range(PARTS):
        part = slice(i * step, (i + 1) * step)
        modes_ref[part, :] = dot(second[part, :], both, HIGHEST)
        copies.append(
            pltpu.make_async_copy(modes_ref.at[part, :], modes_hbm.at[part, :], sem.at[2 + i])
        )
        copies[-1].start()
        if i == 0:
            factor_ref[...] = dot(u_ref[...], upper_one, HIGHEST)
            copies.append(pltpu.make_async_copy(factor_ref, factor_hbm, sem.at[1]))
            copies[-1].start()
    for copy in copies:
        copy.wait()


def finish(sums, snapshots, basis):
    rows = snapshots.shape[0]
    square = pltpu.VMEM((N, N), F32)
    return pl.pallas_call(
        final_kernel,
        out_shape=(
            jax.ShapeDtypeStruct((rows, N), F32),
            jax.ShapeDtypeStruct((N, N), F32),
            jax.ShapeDtypeStruct((N, N), F32),
        ),
        out_specs=(pl.BlockSpec(memory_space=pltpu.HBM),) * 3,
        scratch_shapes=[pltpu.VMEM((rows, N), F32)]
        + [square] * 4
        + [pltpu.SemaphoreType.DMA((2 + PARTS,)), pltpu.VMEM((TILES, TILE * TILE, N), F32)],
        compiler_params=pltpu.CompilerParams(vmem_limit_bytes=48 << 20),
    )(sums, snapshots, basis)


def body(snapshots, basis):
    group, many = lax.axis_size("grp"), lax.axis_size("dev")
    local = local_products(snapshots, basis, group * many)
    parts = lax.all_to_all(local, "dev", 0, 0)
    mine = sum_and_copy(parts, group)
    parts = lax.all_to_all(mine, "grp", 0, 0)
    mine = sum_and_copy(parts, many)
    sums = lax.all_to_all(mine, "dev", 0, 0)
    return finish(sums, snapshots, basis)


def solution(mesh):
    return jax.shard_map(
        body,
        mesh=mesh,
        in_specs=(P(("grp", "dev"), None), P(("grp", "dev"), None)),
        out_specs=(P(("grp", "dev"), None), P(), P()),
        check_vma=False,
    )
```

```python
import functools

import jax
import jax.numpy as jnp
from jax import lax
from jax.experimental import pallas as pl
from jax.experimental.pallas import tpu as pltpu
from jax.sharding import PartitionSpec as P

HIGHEST = lax.Precision.HIGHEST
F32, BF16 = jnp.float32, jnp.bfloat16
N = 128
TILE = 8
TILES = N // TILE


def two_sum(a, b):
    s = a + b
    t = s - a
    return s, (a - (s - t)) + (b - t)


def pair_sum(a, b):
    s, e = two_sum(a[0], b[0])
    return s, e + (a[1] + b[1])


def normal(a):
    s = a[0] + a[1]
    return s, a[1] - (s - a[0])


def dot_t(a, b, precision=None):
    return lax.dot_general(
        a, b, (((0,), (0,)), ((), ())), precision=precision, preferred_element_type=F32
    )


def dot(a, b, precision=None):
    return jnp.dot(a, b, precision=precision, preferred_element_type=F32)


def slices(hi, lo, axis, count, shift):
    step = jnp.max(jnp.abs(hi), axis=axis, keepdims=True) * (2.0**shift)
    first = (hi + step) - step
    rest = hi - first
    step = step * 2.0**-8
    second = (rest + step) - step
    rest = rest - second
    if lo is not None:
        rest = rest + lo
    out = [first.astype(BF16), second.astype(BF16)]
    while len(out) < count:
        part = rest.astype(BF16)
        rest = rest - part.astype(F32)
        out.append(part)
    return out


def exact_dot(left, right):
    wide = jnp.concatenate(left, axis=1)
    tall = jnp.concatenate(right[::-1], axis=0)
    n = len(left)
    terms = [dot(wide[:, : N * k], tall[N * (n - k) :, :]) for k in range(1, n + 1)]
    low = terms[-1]
    for t in terms[-2:1:-1]:
        low = low + t
    s, e = two_sum(terms[0], terms[1])
    return s, e + low


def grid(rows=N):
    return (
        lax.broadcasted_iota(jnp.int32, (rows, N), 0),
        lax.broadcasted_iota(jnp.int32, (rows, N), 1),
    )


def put_diagonal(rest, diagonal):
    row, col = grid(N // 2)
    near = pltpu.roll(diagonal[N // 2 :, :], N - N // 4, 1)
    far = pltpu.roll(diagonal[: N // 2, :], N // 2, 1)
    top = jnp.where(col == row + N // 4, near, rest[: N // 2, :])
    top = jnp.where(col == row + N // 2, far, top)
    return jnp.concatenate([top, rest[N // 2 :, :]], axis=0)


def take_diagonal(rest):
    row, col = grid(N // 2)
    top = rest[: N // 2, :]
    near, far = col == row + N // 4, col == row + N // 2
    first = pltpu.roll(jnp.where(far, top, 0.0), N // 2, 1)
    last = pltpu.roll(jnp.where(near, top, 0.0), N // 4, 1)
    top = jnp.where(near | far, 0.0, top)
    return (
        jnp.concatenate([first, last], axis=0),
        jnp.concatenate([top, rest[N // 2 :, :]], axis=0),
    )


def pack(hi, lo):
    hi, lo = hi.reshape(TILES, TILE, N), lo.reshape(TILES, TILE, N)
    upper = lax.broadcasted_iota(jnp.int32, hi.shape, 1) < TILE // 2
    even = jnp.where(upper, hi, pltpu.roll(lo, TILE // 2, 1))
    odd = jnp.where(upper, pltpu.roll(hi, TILE // 2, 1), lo)
    return jnp.stack([even, odd], axis=1).reshape(2 * TILES, TILE, N)


def unpack(pieces):
    pieces = pieces.reshape(TILES, 2, TILE, N)
    even, odd = pieces[:, 0], pieces[:, 1]
    upper = lax.broadcasted_iota(jnp.int32, even.shape, 1) < TILE // 2
    hi = jnp.where(upper, even, pltpu.roll(odd, TILE // 2, 1))
    lo = jnp.where(upper, pltpu.roll(even, TILE // 2, 1), odd)
    return hi.reshape(N, N), lo.reshape(N, N)


def local_kernel(share, total, z_ref, out_ref):
    a, b, c, d = slices(z_ref[...], None, 0, 4, 17)
    main = dot_t(a, a)
    low_1 = dot_t(a, b)
    low_2 = dot_t(a, c) + 0.5 * dot_t(b, b)
    low_3 = dot_t(a, d) + dot_t(b, c)
    low_4 = dot_t(b, d) + 0.5 * dot_t(c, c)
    half = low_1 + (low_2 + (low_3 + low_4))
    hi, lo = two_sum(main, half + half.T)
    hi, lo = hi * (1.0 / total), lo * (1.0 / total)
    row, col = grid()
    diagonal = jnp.where(row == col, (hi[:N, :N] - share) + lo[:N, :N], 0.0)
    mixed_hi = jnp.where(row < col, hi[:N, :N], hi[N:, N:])
    mixed_lo = put_diagonal(jnp.where(row < col, lo[:N, :N], lo[N:, N:]), diagonal)
    out_ref[: 2 * TILES] = pack(mixed_hi, mixed_lo)
    out_ref[2 * TILES :] = pack(hi[:N, N:], lo[:N, N:])


def local_products(snapshots, basis, devices):
    rows = snapshots.shape[0]
    total = rows * devices
    return pl.pallas_call(
        functools.partial(local_kernel, 1.0 / devices, total),
        out_shape=jax.ShapeDtypeStruct((4 * TILES, TILE, N), F32),
        compiler_params=pltpu.CompilerParams(vmem_limit_bytes=32 << 20),
    )(jnp.concatenate([basis, snapshots], axis=1))


def sum_kernel(in_ref, out_ref):
    parts = [(in_ref[i], None) for i in range(in_ref.shape[0])]
    while len(parts) > 1:
        added = []
        for (a, a_left), (b, b_left) in zip(parts[::2], parts[1::2]):
            s, left = two_sum(a, b)
            if a_left is not None:
                left = left + (a_left + b_left)
            added.append((s, left))
        parts = added
    s, left = parts[0]
    lower = lax.broadcasted_iota(jnp.int32, s.shape, 0) >= TILE // 2
    s = s + jnp.where(lower, pltpu.roll(left, TILE // 2, 0), 0.0)
    for i in range(out_ref.shape[0]):
        out_ref[i] = s


def sum_and_copy(parts, copies):
    return pl.pallas_call(
        sum_kernel,
        out_shape=jax.ShapeDtypeStruct((copies, TILE, N), F32),
        compiler_params=pltpu.CompilerParams(vmem_limit_bytes=32 << 20),
    )(parts)


def spread_row(tile, k):
    return jnp.broadcast_to(tile[k : k + 1, :], (TILE, N))


def spread_lane(tile, j):
    return jnp.broadcast_to(tile[:, j : j + 1], (TILE, N))


AHEAD = 1


def spread_ref(ref, p, k):
    return jnp.broadcast_to(ref[p, k : k + 1, :], (TILE, N))


def factor_inverse(gram, scr):
    sub = lax.broadcasted_iota(jnp.int32, (TILE, N), 0)
    lane = lax.broadcasted_iota(jnp.int32, (TILE, N), 1)
    work = [gram[q * TILE : (q + 1) * TILE, :] for q in range(TILES)]
    upper, inverse = [], []
    for p in range(TILES):
        at, after = p * TILE, range(p + 1, TILES)
        near, far = after[:AHEAD], after[AHEAD:]
        d = {}
        for j in range(TILE):
            scr[p, TILE * j : TILE * j + TILE, :] = spread_lane(work[p], at + j)
            for i in range(j + 1):
                d[i, j] = spread_ref(scr, p, TILE * j + i)
        below = {(q, j): spread_lane(work[q], at + j) for q in near for j in range(TILE)}
        right = lane >= at + TILE
        block = (lane >= at) & (lane < at + TILE)
        for q in after:
            work[q] = jnp.where(block, 0.0, work[q])
        left = jnp.where(lane < at, work[p], jnp.where(lane == at + sub, 1.0, 0.0))
        scr[p, TILE * TILE : TILE * TILE + TILE, :] = work[p]
        scr[p, TILE * TILE + TILE :, :] = left
        rows = [
            (spread_ref(scr, p, TILE * TILE + k), spread_ref(scr, p, TILE * TILE + TILE + k))
            for k in range(TILE)
        ]
        new = [jnp.zeros((TILE, N), F32)] * 2
        for k in range(TILE):
            scale = lax.rsqrt(d[k, k])
            for j in range(k + 1, TILE):
                d[k, j] = d[k, j] * scale
            for i in range(k + 1, TILE):
                for j in range(i, TILE):
                    d[i, j] = d[i, j] - d[k, i] * d[k, j]
            row = (rows[k][0] * scale, rows[k][1] * scale)
            for i in range(k + 1, TILE):
                rows[i] = tuple(a - d[k, i] * b for a, b in zip(rows[i], row))
            finished = jnp.where(right, *row)
            for q in near:
                m = below[q, k] * scale
                for j in range(k + 1, TILE):
                    below[q, j] = below[q, j] - m * d[k, j]
                work[q] = work[q] - m * finished
            for q in far:
                m = jnp.take_along_axis(row[0], sub + q * TILE, axis=1)
                work[q] = work[q] - m * finished
            new = [jnp.where(sub == k, a, b) for a, b in zip(row, new)]
        upper.append(jnp.where(lane >= at + sub, new[0], 0.0))
        inverse.append(jnp.where(right, 0.0, new[1]))
    return jnp.concatenate(upper, axis=0), jnp.concatenate(inverse, axis=0)


def power_near(value):
    p, q = jnp.ones_like(value), jnp.ones_like(value)
    for k in (4, 2, 1):
        large = (value * p) * p > 2.0 ** (2 * k - 1)
        p, q = jnp.where(large, p * 2.0**-k, p), jnp.where(large, q * 2.0**k, q)
    for k in (32, 16, 8, 4, 2, 1):
        small = (value * p) * p < 2.0 ** (1 - 2 * k)
        p, q = jnp.where(small, p * 2.0**k, p), jnp.where(small, q * 2.0**-k, q)
    return p, q


def three_square(a):
    hi = a.astype(BF16)
    lo = (a - hi.astype(F32)).astype(BF16)
    return lax.dot_general(
        jnp.concatenate([hi, hi, lo], 1),
        jnp.concatenate([hi, lo, hi], 1),
        (((1,), (1,)), ((), ())),
        preferred_element_type=F32,
    )


def three_dot(left, right):
    l1, r1 = left.astype(BF16), right.astype(BF16)
    l2 = (left - l1.astype(F32)).astype(BF16)
    r2 = (right - r1.astype(F32)).astype(BF16)
    return dot(jnp.concatenate([l1, l1, l2], 1), jnp.concatenate([r1, r2, r1], 0))


NEAR = 2.0**-4
TURNS = 4


def near_factor(off, inv_one):
    row, col = grid()
    weight = jnp.where(row > col, 1.0, jnp.where(row == col, 0.5, 0.0))
    low = off * weight
    for _ in range(TURNS):
        low = (off - three_square(low)) * weight
    n = low.T
    first = inv_one - dot(inv_one, n, HIGHEST)
    n2 = three_dot(n, n)
    n2 = n2 + three_dot(n2, n2)
    return jnp.where(row == col, 1.0, 0.0) + n, first + three_dot(first, n2)


PARTS = 4


def final_kernel(sums_ref, snap_ref, basis_ref, modes_hbm, factor_hbm, coef_hbm,
                 modes_ref, factor_ref, coef_ref, u_ref, t_ref, sem, scr):
    row, col = grid()
    mixed_hi, mixed_lo = unpack(sums_ref[: 2 * TILES])
    cross = unpack(sums_ref[2 * TILES :])
    diagonal, mixed_lo = take_diagonal(mixed_lo)
    turned_hi, turned_lo = mixed_hi.T, mixed_lo.T
    one = jnp.where(row == col, 1.0, 0.0)
    one_hi, one_lo = two_sum(one, diagonal)
    basis_gram = (
        jnp.where(row == col, one_hi, jnp.where(row < col, mixed_hi, turned_hi)),
        jnp.where(row == col, one_lo, jnp.where(row < col, mixed_lo, turned_lo)),
    )
    snap_gram = (
        jnp.where(row < col, turned_hi, mixed_hi),
        jnp.where(row < col, turned_lo, mixed_lo),
    )
    coef_two = cross[0] - dot(basis_gram[0], cross[0], HIGHEST)
    coef = cross[0] + coef_two
    coef_ref[...] = coef
    coef_copy = pltpu.make_async_copy(coef_ref, coef_hbm, sem.at[0])
    coef_copy.start()
    second = snap_ref[...] - dot(basis_ref[...], coef, HIGHEST)

    g_c = exact_dot(slices(*basis_gram, 1, 5, 16), slices(coef, None, 0, 5, 16))
    held = pair_sum((2.0 * cross[0], 2.0 * cross[1]), (-g_c[0], -g_c[1]))
    held = normal(held)
    c_h = exact_dot(slices(coef.T, None, 1, 5, 16), slices(*held, 0, 5, 16))
    c_h = pair_sum((0.5 * c_h[0], 0.5 * c_h[1]), (0.5 * c_h[0].T, 0.5 * c_h[1].T))
    gram_one = normal(pair_sum(snap_gram, (-c_h[0], -c_h[1])))

    upper_one, inv_one_t = factor_inverse(gram_one[0], scr)
    inv_one = inv_one_t.T
    diagonal = jnp.where(row == col, gram_one[0], 0.0)
    across, back_across = power_near(jnp.sum(diagonal, axis=0, keepdims=True))
    down, back_down = power_near(jnp.sum(diagonal, axis=1, keepdims=True))
    scaled = tuple((part * across) * down for part in gram_one)
    g_i = exact_dot(slices(*scaled, 1, 5, 16), slices(inv_one * back_down, None, 0, 5, 16))
    g_i = normal(g_i)
    i_g_i = exact_dot(slices(inv_one_t * back_across, None, 1, 5, 16), slices(*g_i, 0, 5, 16))
    off = (i_g_i[0] - one) + i_g_i[1]
    is_near = jnp.sum(off * off) <= NEAR * NEAR

    u_ref[...], t_ref[...] = near_factor(off, inv_one)

    @pl.when(jnp.logical_not(is_near))
    def _():
        upper, inv_t = factor_inverse(one + off, scr)
        u_ref[...] = upper
        t_ref[...] = dot(inv_one, inv_t.T, HIGHEST)

    both = t_ref[...]
    copies = [coef_copy]
    step = modes_ref.shape[0] // PARTS
    for i in range(PARTS):
        part = slice(i * step, (i + 1) * step)
        modes_ref[part, :] = dot(second[part, :], both, HIGHEST)
        copies.append(
            pltpu.make_async_copy(modes_ref.at[part, :], modes_hbm.at[part, :], sem.at[2 + i])
        )
        copies[-1].start()
        if i == 0:
            factor_ref[...] = dot(u_ref[...], upper_one, HIGHEST)
            copies.append(pltpu.make_async_copy(factor_ref, factor_hbm, sem.at[1]))
            copies[-1].start()
    for copy in copies:
        copy.wait()


def finish(sums, snapshots, basis):
    rows = snapshots.shape[0]
    square = pltpu.VMEM((N, N), F32)
    return pl.pallas_call(
        final_kernel,
        out_shape=(
            jax.ShapeDtypeStruct((rows, N), F32),
            jax.ShapeDtypeStruct((N, N), F32),
            jax.ShapeDtypeStruct((N, N), F32),
        ),
        out_specs=(pl.BlockSpec(memory_space=pltpu.HBM),) * 3,
        scratch_shapes=[pltpu.VMEM((rows, N), F32)]
        + [square] * 4
        + [pltpu.SemaphoreType.DMA((2 + PARTS,)), pltpu.VMEM((TILES, TILE * (TILE + 2), N), F32)],
        compiler_params=pltpu.CompilerParams(vmem_limit_bytes=48 << 20),
    )(sums, snapshots, basis)


def body(snapshots, basis):
    group, many = lax.axis_size("grp"), lax.axis_size("dev")
    local = local_products(snapshots, basis, group * many)
    parts = lax.all_to_all(local, "dev", 0, 0)
    mine = sum_and_copy(parts, group)
    parts = lax.all_to_all(mine, "grp", 0, 0)
    mine = sum_and_copy(parts, many)
    sums = lax.all_to_all(mine, "dev", 0, 0)
    return finish(sums, snapshots, basis)


def solution(mesh):
    return jax.shard_map(
        body,
        mesh=mesh,
        in_specs=(P(("grp", "dev"), None), P(("grp", "dev"), None)),
        out_specs=(P(("grp", "dev"), None), P(), P()),
        check_vma=False,
    )
```
